512 devices in a mesh: grp: 16 (over y, x_lo), seq: 32 (over x_hi, z, core).
Axes of the slice: x: 4 (x_hi: 2, x_lo: 2; x = x_hi * 2 + x_lo), y: 8, z: 8, core: 2. Of those that a mesh axis runs over, the one named last changes fastest.
Arguments:
- queries: bfloat16 [512, 2, 64, 128], P(('grp', 'seq')), may hold values from -40 to 40
- root_keys: bfloat16 [16384, 8, 128], P(('grp', 'seq')), may hold values from -12 to 12
- root_values: bfloat16 [16384, 8, 128], P(('grp', 'seq')), may hold values from -4 to 4
- branch_keys: bfloat16 [16, 8192, 8, 128], P('grp', 'seq'), may hold values from -12 to 12
- branch_values: bfloat16 [16, 8192, 8, 128], P('grp', 'seq'), may hold values from -4 to 4
- suffix_keys: bfloat16 [512, 512, 8, 128], P(('grp', 'seq')), may hold values from -12 to 12
- suffix_values: bfloat16 [512, 512, 8, 128], P(('grp', 'seq')), may hold values from -4 to 4
- new_keys: bfloat16 [512, 2, 8, 128], P(('grp', 'seq')), may hold values from -12 to 12
- new_values: bfloat16 [512, 2, 8, 128], P(('grp', 'seq')), may hold values from -4 to 4
- branch_of: int32 [512], replicated, may hold values from 0 to 15, as said below
- owner: int32 [16], replicated, may hold values from 0 to 15, as said below
- suffix_len: int32 [512], P(('grp', 'seq')), may hold values from 1 to 512, 131072 in all
Outputs:
- attended: bfloat16 [512, 2, 64, 128], P(('grp', 'seq'))
The draws below stay inside these ranges and needn't reach their ends.
Inputs may be any that keep to these rules, and one draw needn't show every extreme that they name: `branch_of`: among the 16 requests g * 32 + s of one s, at most 2 read the same branch; some branch is read by exactly 2 of them for every s. Every branch is read by some request. `owner`: each group holds a different branch. `suffix_len`: some request uses all 512 positions.
All inputs are finite; a program needn't handle non-finite values. No bound on the sum of `suffix_len` on one device may be relied on, other than what follows from the above.
Results may differ from the reference program's by a relative error of at most 0.0025.
Values may be sent and summed in bfloat16 or wider, within the bound.
No kernel may reach another device: no remote copies, remote signals or barrier semaphores. Data moves between devices by JAX's collectives and lax.ppermute only.
A program may use at most 128 MiB of HBM per device.

```python
import math
import jax
import jax.numpy as jnp
import numpy as np
from jax import lax

QH = 64
KVH = 8
HD = 128
STEPS = 2
CAP = 2
BR_DEV = 256
SUF = 512
NB = 16
REQUESTS = 512
ROOT = 16384
BR_LEN = 8192
N_GRP = 16
N_SEQ = 32


def shared_keys(key):
    return jnp.clip(3.0 * jax.random.normal(key, (ROOT, KVH, HD), jnp.float32), -12.0, 12.0)


def draw_root_keys(key, part):
    return shared_keys(key).astype(jnp.bfloat16)


def draw_queries(key, part):
    key = jax.random.fold_in(key, 7)
    key_drawn = jax.random.fold_in(key, 0)
    drawn = jnp.clip(jax.random.normal(key_drawn, (REQUESTS, STEPS, QH, HD), jnp.float32), -4.0, 4.0)
    return drawn.astype(jnp.bfloat16)


def draw_owner(key, part):
    key = jax.random.fold_in(key, 11)
    return jax.random.permutation(key, NB).astype(jnp.int32)


def draw_branch_of(key, part):
    key = jax.random.fold_in(key, 5)
    key_warm, key_hottest, key_jitter, key_shuffle = jax.random.split(key, 4)
    warmth = jax.random.randint(key_warm, (NB,), 0, 4)
    hottest = jax.random.randint(key_hottest, (), 0, NB)
    warmth = jnp.where(jnp.arange(NB) == hottest, 64, warmth)
    item_ids = jnp.arange(NB * CAP)
    item_branch = item_ids // CAP
    row_ids = jnp.arange(N_SEQ)
    forced = (item_branch[None, :] == row_ids[:, None] % NB).astype(jnp.int32) * 32
    jitter = jax.random.randint(key_jitter, (N_SEQ, NB * CAP), 0, 6)
    ranking = ((warmth[item_branch][None, :] + forced) * 8 + jitter) * (NB * CAP) + item_ids[None, :]
    ordered = jnp.argsort(-ranking, axis=1)[:, :N_GRP]
    chosen = item_branch[ordered]
    shuffle_keys = jax.random.randint(key_shuffle, (N_SEQ, N_GRP), 0, 1048576) * N_GRP + jnp.arange(N_GRP)[None, :]
    shuffle = jnp.argsort(shuffle_keys, axis=1)
    placed = jnp.take_along_axis(chosen, shuffle, axis=1)
    return placed.T.reshape(N_GRP * N_SEQ).astype(jnp.int32)


def levels(rng, extent, shards, least, largest):
    level, own = 1.0, jax.random.fold_in(rng, 6)
    for position, blocks in shards:
        heights = jnp.exp(jax.random.uniform(jax.random.fold_in(own, position), (blocks,), jnp.float32, least / len(shards), largest / len(shards)))
        level = level * jnp.repeat(heights, extent[position] // blocks).reshape([-1 if axis == position else 1 for axis in range(len(extent))])
    return level


def length_profile(number_of, total, limit, slope):
    loads = [(1 << 20) // math.isqrt(rank ** slope) + 1 for rank in range(2, number_of + 1)]
    surplus, holding = total - limit - (number_of - 1), [1] * (number_of - 1)
    while surplus > 0:
        candidates = [i for i in range(number_of - 1) if holding[i] < limit]
        mass, left = sum([loads[i] for i in candidates]), surplus
        for i in candidates:
            extra = min(limit - holding[i], max(1, left * loads[i] // mass), surplus)
            holding[i] = holding[i] + extra
            surplus = surplus - extra
    return np.array([limit] + holding)


def ragged(key, count, total, reach, slope):
    if count == 2:
        one = jax.random.randint(key, (), max(1, total - reach), min(reach, total - 1) + 1)
        return jnp.stack([one, total - one])
    lengths = jnp.asarray(length_profile(count, total, reach, slope), jnp.int32)
    twos = (count - 1) // 2
    donor, sink = lengths[1:1 + 2 * twos:2], lengths[2:2 + 2 * twos:2]
    margin = jnp.minimum(donor - 1, reach - sink)
    passed = jax.random.randint(jax.random.fold_in(key, 1), (twos,), 0, 1 << 20) % (margin + 1)
    lengths = lengths.at[1:1 + 2 * twos:2].set(donor - passed).at[2:2 + 2 * twos:2].set(sink + passed)
    return lengths[jax.random.permutation(jax.random.fold_in(key, 2), count)]


def normal_values(own_key, dims, deviation, most, cuts=(), dtype=jnp.bfloat16):
    entries = jax.random.normal(own_key, dims, jnp.float32) * deviation
    if len(cuts) > 0:
        entries = levels(own_key, dims, cuts, -0.22, 0.18) * entries
    return jnp.clip(entries, min=-most, max=most).astype(dtype)


def setup_inputs(seed: int = 0) -> dict:
    seeds = jax.random.split(jax.random.key(seed), 13)
    queries = draw_queries(jax.random.fold_in(seeds[12], 71), 0)
    root_keys = draw_root_keys(jax.random.fold_in(seeds[12], 71), 0)
    root_values = normal_values(seeds[2], (ROOT, KVH, HD), 1.0, 4.0, ((0, 512),))
    branch_keys = normal_values(seeds[3], (NB, BR_LEN, KVH, HD), 3.0, 12.0, ((0, 16), (1, 32)))
    branch_values = normal_values(seeds[4], (NB, BR_LEN, KVH, HD), 1.0, 4.0, ((0, 16), (1, 32)))
    suffix_keys = normal_values(seeds[5], (REQUESTS, SUF, KVH, HD), 3.0, 12.0, ((0, 512),))
    suffix_values = normal_values(seeds[6], (REQUESTS, SUF, KVH, HD), 1.0, 4.0, ((0, 512),))
    new_keys = normal_values(seeds[7], (REQUESTS, STEPS, KVH, HD), 3.0, 12.0, ((0, 512),))
    new_values = normal_values(seeds[8], (REQUESTS, STEPS, KVH, HD), 1.0, 4.0, ((0, 512),))
    branch_of = draw_branch_of(jax.random.fold_in(seeds[12], 71), 0)
    owner = draw_owner(jax.random.fold_in(seeds[12], 71), 0)
    suffix_len = ragged(seeds[11], REQUESTS, REQUESTS * SUF // 2, SUF, 2).astype(jnp.int32)
    return {"queries": queries, "root_keys": root_keys, "root_values": root_values, "branch_keys": branch_keys, "branch_values": branch_values, "suffix_keys": suffix_keys, "suffix_values": suffix_values, "new_keys": new_keys, "new_values": new_values, "branch_of": branch_of, "owner": owner, "suffix_len": suffix_len}


def softmax_piece(query_here, key_rows, value_rows, visible):
    scaling = 1.0 / math.sqrt(key_rows.shape[-1])
    scores = jnp.einsum('sjgd,ljd->sjgl', query_here, key_rows.astype(jnp.float32)) * scaling
    scores = jnp.where(visible, scores, -jnp.inf)
    highest = lax.optimization_barrier(jnp.max(scores, axis=-1))
    weights = jnp.exp(scores - highest[..., None])
    rounded = lax.optimization_barrier(weights.astype(jnp.bfloat16)).astype(jnp.float32)
    numerator = jnp.einsum('sjgl,ljd->sjgd', rounded, value_rows.astype(jnp.float32))
    return (highest, numerator, lax.optimization_barrier(jnp.sum(weights, axis=-1)))

def combine_pieces(pieces):
    overall = pieces[0][0]
    for entry in pieces[1:]:
        overall = jnp.maximum(overall, entry[0])
    numerator = jnp.zeros(pieces[0][1].shape, jnp.float32)
    denominator = jnp.zeros(pieces[0][2].shape, jnp.float32)
    for entry in pieces:
        factor = jnp.exp(entry[0] - overall)
        numerator = numerator + factor[..., None] * entry[1]
        denominator = denominator + factor * entry[2]
    return (numerator / denominator[..., None]).astype(jnp.bfloat16)

def reference(queries, root_keys, root_values, branch_keys, branch_values, suffix_keys, suffix_values, new_keys, new_values, branch_of, owner, suffix_len):
    per_group = QH // KVH
    scaling = 1.0 / math.sqrt(HD)
    query_rows = queries.astype(jnp.float32).reshape(REQUESTS, STEPS, KVH, per_group, HD)
    block_size = math.gcd(ROOT, 512)
    key_blocks = root_keys.reshape(ROOT // block_size, block_size, KVH, HD)
    value_blocks = root_values.reshape(ROOT // block_size, block_size, KVH, HD)

    def block_max(running, key_block):
        scores = jnp.einsum('rsjgd,ljd->rsjgl', query_rows, key_block.astype(jnp.float32)) * scaling
        return (jnp.maximum(running, lax.optimization_barrier(jnp.max(scores, axis=-1))), None)
    start_high = jnp.full(query_rows.shape[:4], -jnp.inf, jnp.float32)
    root_high, _ = lax.scan(block_max, start_high, key_blocks)

    def block_sum(carry, blocks):
        key_block, value_block = blocks
        scores = jnp.einsum('rsjgd,ljd->rsjgl', query_rows, key_block.astype(jnp.float32)) * scaling
        weights = jnp.exp(scores - root_high[..., None])
        rounded = lax.optimization_barrier(weights.astype(jnp.bfloat16)).astype(jnp.float32)
        numerator = carry[0] + jnp.einsum('rsjgl,ljd->rsjgd', rounded, value_block.astype(jnp.float32))
        return ((numerator, carry[1] + lax.optimization_barrier(jnp.sum(weights, axis=-1))), None)
    start_sums = (jnp.zeros(query_rows.shape, jnp.float32), jnp.zeros(query_rows.shape[:4], jnp.float32))
    (root_num, root_den), _ = lax.scan(block_sum, start_sums, (key_blocks, value_blocks))
    slot_of = owner[branch_of].astype(jnp.int32)
    positions = jnp.arange(SUF + STEPS)
    step_ids = jnp.arange(STEPS)

    def per_request(inputs):
        query_here, slot, suffix_key, suffix_value, fresh_key, fresh_value, length, high_here, num_here, den_here = inputs
        branch_key = lax.dynamic_index_in_dim(branch_keys, slot, 0, keepdims=False).reshape(N_SEQ, BR_DEV, KVH, HD)
        branch_value = lax.dynamic_index_in_dim(branch_values, slot, 0, keepdims=False).reshape(N_SEQ, BR_DEV, KVH, HD)
        block_high, block_num, block_den = jax.vmap(lambda kb, vb: softmax_piece(query_here, kb, vb, True))(branch_key, branch_value)
        branch_high = lax.optimization_barrier(jnp.max(block_high, axis=0))
        factor = jnp.exp(block_high - branch_high[None])
        branch_piece = (branch_high, lax.optimization_barrier(jnp.sum(factor[..., None] * block_num, axis=0)), lax.optimization_barrier(jnp.sum(factor * block_den, axis=0)))
        visible = jnp.where(positions[None, :] < SUF, positions[None, :] < length, positions[None, :] - SUF <= step_ids[:, None])
        local_key = jnp.concatenate([suffix_key, fresh_key], axis=0)
        local_value = jnp.concatenate([suffix_value, fresh_value], axis=0)
        local_piece = softmax_piece(query_here, local_key, local_value, visible[:, None, None, :])
        return combine_pieces([(high_here, num_here, den_here), branch_piece, local_piece])
    attended = lax.map(per_request, (query_rows, slot_of, suffix_keys, suffix_values, new_keys, new_values, suffix_len, root_high, root_num, root_den))
    return attended.reshape(REQUESTS, STEPS, QH, HD)
```

```python
import functools
import math

import jax
import jax.numpy as jnp
from jax import lax
from jax.experimental import pallas as pl
from jax.experimental.pallas import tpu as pltpu
from jax.sharding import Mesh, PartitionSpec as P

CAP = 2
PAD = 8
LOW = -1e30
VMEM_LIMIT = 48 * 1024 * 1024
NT = (((1,), (1,)), ((), ()))


def scores_of(rows, keys):
    raw = lax.dot_general(rows, keys, NT, preferred_element_type=jnp.float32)
    return raw * (1.0 / math.sqrt(keys.shape[-1]))


def times_values(weights, values):
    return jnp.dot(weights.astype(jnp.bfloat16), values, preferred_element_type=jnp.float32)


def put_lse(out_ref, lead, lse, per_head, head):
    lanes = out_ref.shape[-1]
    lse = jnp.broadcast_to(lse, (lse.shape[0], lanes))
    row = lax.broadcasted_iota(jnp.int32, lse.shape, 0)
    col = lax.broadcasted_iota(jnp.int32, lse.shape, 1)
    lse = jnp.where(col == head * per_head + row % per_head, lse, 0.0)
    flat = jnp.sum(lse.reshape(-1, per_head, lanes), axis=1, keepdims=True)
    out_ref[lead, lanes:, :] += jnp.broadcast_to(flat, (flat.shape[0], PAD, lanes))


def split_lse(lse):
    coarse = jnp.round(lse * 0.25) * 4.0
    rest = lse - coarse
    middle = jnp.round(rest * 512.0) * (1.0 / 512.0)
    return coarse, middle, rest - middle


def split_tail(out_ref, lead):
    lanes = out_ref.shape[-1]
    lse = out_ref[lead, lanes:, :]
    coarse, middle, fine = split_lse(lse)
    row = lax.broadcasted_iota(jnp.int32, lse.shape, lse.ndim - 2)
    out_ref[lead, lanes:, :] = jnp.where(
        row == 0, coarse, jnp.where(row == 1, middle, jnp.where(row == 2, fine, 0.0))
    )


def join_lse(tail):
    return tail[..., 0, :] + tail[..., 1, :] + tail[..., 2, :]


def local_kernel(heads, len_ref, q_ref, k_ref, v_ref, nk_ref, nv_ref, out_ref):
    rows = q_ref.shape[0]
    per_head = rows // heads
    q = q_ref[...]
    far = scores_of(q, k_ref[...])
    row = lax.broadcasted_iota(jnp.int32, far.shape, 0)
    col = lax.broadcasted_iota(jnp.int32, far.shape, 1)
    seen = (col % heads == row // per_head) & (col < len_ref[0] * heads)
    far = jnp.where(seen, far, LOW)
    near = scores_of(q, nk_ref[...])
    row = lax.broadcasted_iota(jnp.int32, near.shape, 0)
    col = lax.broadcasted_iota(jnp.int32, near.shape, 1)
    steps = near.shape[1] // heads
    step = (row % per_head) // (per_head // steps)
    seen = (col % heads == row // per_head) & (col // heads <= step)
    near = jnp.where(seen, near, LOW)
    high = jnp.maximum(
        jnp.max(far, axis=1, keepdims=True), jnp.max(near, axis=1, keepdims=True)
    )
    far = jnp.exp(far - high)
    near = jnp.exp(near - high)
    den = jnp.sum(far, axis=1, keepdims=True) + jnp.sum(near, axis=1, keepdims=True)
    num = times_values(far, v_ref[...]) + times_values(near, nv_ref[...])
    out_ref[:rows, :] = num / den
    lse = jnp.broadcast_to(high + jnp.log(den), (rows, rows))
    row = lax.broadcasted_iota(jnp.int32, (rows, rows), 0)
    col = lax.broadcasted_iota(jnp.int32, (rows, rows), 1)
    flat = jnp.sum(jnp.where(row == col, lse, 0.0), axis=0, keepdims=True)
    out_ref[rows:, :] = jnp.broadcast_to(flat, (PAD, rows))


def select_kernel(idx_ref, peer_ref, out_ref):
    out_ref[...] = jnp.broadcast_to(peer_ref[...][None], out_ref.shape)


def branch_kernel(q_ref, own_ref, twin_ref, out_ref):
    head = pl.program_id(0)
    slots, per_head, dim = q_ref.shape
    lanes = out_ref.shape[-1]

    @pl.when(head == 0)
    def _():
        out_ref[:, lanes:, :] = jnp.zeros((slots, PAD, lanes), jnp.float32)

    step = min(16, slots)
    for start in range(0, slots, step):
        lead = slice(start, start + step)
        rows = step * per_head
        q = q_ref[lead].reshape(rows, dim)
        found = []
        for ref in (own_ref, twin_ref):
            scores = scores_of(q, ref[0, 0])
            high = jnp.max(scores, axis=1, keepdims=True)
            weights = jnp.exp(scores - high)
            den = jnp.sum(weights, axis=1, keepdims=True)
            found.append((high, den, times_values(weights, ref[1, 0])))
        (high_a, den_a, num_a), (high_b, den_b, num_b) = found
        high = jnp.maximum(high_a, high_b)
        factor_a = jnp.exp(high_a - high)
        factor_b = jnp.exp(high_b - high)
        den = factor_a * den_a + factor_b * den_b
        num = num_a * (factor_a / den) + num_b * (factor_b / den)
        place = pl.ds(pl.multiple_of(head * per_head, per_head), per_head)
        out_ref[lead, place, :] = num.reshape(step, per_head, dim)
        put_lse(out_ref, lead, high + jnp.log(den), per_head, head)

    @pl.when(head == pl.num_programs(0) - 1)
    def _():
        split_tail(out_ref, slice(0, slots))


def root_kernel(count, *refs):
    q_refs, block_refs, out_refs = refs[:2], refs[2 : 2 + count], refs[2 + count :]
    head = pl.program_id(0)
    requests, per_head, dim = q_refs[0].shape
    rows = requests * per_head
    half = block_refs[0].shape[2] // 2
    keys = jnp.concatenate([r[i, 0, :half, :] for r in block_refs for i in range(2)], axis=0)
    values = jnp.concatenate([r[i, 0, half:, :] for r in block_refs for i in range(2)], axis=0)
    for q_ref, out_ref in zip(q_refs, out_refs):
        lanes = out_ref.shape[-1]

        @pl.when(head == 0)
        def _():
            out_ref[:, lanes:, :] = jnp.zeros((requests, PAD, lanes), jnp.float32)

        scores = scores_of(q_ref[...].reshape(rows, dim), keys)
        high = jnp.max(scores, axis=1, keepdims=True)
        weights = jnp.exp(scores - high)
        den = jnp.sum(weights, axis=1, keepdims=True)
        num = times_values(weights, values) / den
        place = pl.ds(pl.multiple_of(head * per_head, per_head), per_head)
        out_ref[:, place, :] = num.reshape(requests, per_head, dim)
        put_lse(out_ref, slice(0, requests), high + jnp.log(den), per_head, head)


def columns(table):
    lanes = table.shape[1]
    rest = jnp.zeros((lanes - table.shape[0], lanes), jnp.float32)
    return jnp.concatenate([table, rest], axis=0).T


def merge_kernel(idx_ref, part_ref, own_ref, twin_ref, out_ref):
    sources, cap, _, lanes = part_ref.shape
    groups = own_ref.shape[0]
    lse_a = own_ref[:, lanes, :]
    lse_b = twin_ref[:, lanes, :]
    high = jnp.maximum(lse_a, lse_b)
    factor_a = jnp.exp(lse_a - high)
    factor_b = jnp.exp(lse_b - high)
    total = factor_a + factor_b
    table = columns(jnp.concatenate([factor_a / total, factor_b / total], axis=0))
    pieces = split_lse(high + jnp.log(total))
    row = lax.broadcasted_iota(jnp.int32, (PAD, lanes), 0)
    for r in range(groups):
        out_ref[r, :lanes, :] = (
            own_ref[r, :lanes, :] * table[:, r : r + 1]
            + twin_ref[r, :lanes, :] * table[:, groups + r : groups + r + 1]
        )
        a, b, c = (jnp.broadcast_to(p[r : r + 1], (PAD, lanes)) for p in pieces)
        out_ref[r, lanes:, :] = jnp.where(
            row == 0, a, jnp.where(row == 1, b, jnp.where(row == 2, c, 0.0))
        )
    for k in range(cap):
        reader = idx_ref[k]

        @pl.when(reader >= 0)
        def _():
            lse = join_lse(part_ref[:, k, lanes:, :])
            near = join_lse(out_ref[reader, lanes:, :])[None]
            high = jnp.maximum(jnp.max(lse, axis=0, keepdims=True), near)
            factor = jnp.exp(lse - high)
            near = jnp.exp(near - high)
            total = jnp.sum(factor, axis=0, keepdims=True) + near
            table = columns(jnp.concatenate([factor / total, near / total], axis=0))
            out = out_ref[reader, :lanes, :] * table[:, sources : sources + 1]
            for source in range(sources):
                out = out + part_ref[source, k, :lanes, :] * table[:, source : source + 1]
            out_ref[reader, :lanes, :] = out
            a, b, c = (jnp.broadcast_to(p, (PAD, lanes)) for p in split_lse(high + jnp.log(total)))
            out_ref[reader, lanes:, :] = jnp.where(
                row == 0, a, jnp.where(row == 1, b, jnp.where(row == 2, c, 0.0))
            )


def final_kernel(part_ref, local_ref, out_ref):
    groups, _, lanes = part_ref.shape
    lse = join_lse(part_ref[:, lanes:, :])
    near = local_ref[lanes : lanes + 1, :]
    high = jnp.maximum(jnp.max(lse, axis=0, keepdims=True), near)
    factor = jnp.exp(lse - high)
    near = jnp.exp(near - high)
    total = jnp.sum(factor, axis=0, keepdims=True) + near
    table = columns(jnp.concatenate([factor / total, near / total], axis=0))
    out = local_ref[:lanes, :] * table[:, groups : groups + 1]
    for source in range(groups):
        out = out + part_ref[source, :lanes, :] * table[:, source : source + 1]
    out_ref[...] = out.astype(out_ref.dtype)


def params():
    return pltpu.CompilerParams(vmem_limit_bytes=VMEM_LIMIT)


def vmem():
    return pl.BlockSpec(memory_space=pltpu.VMEM)


def smem():
    return pl.BlockSpec(memory_space=pltpu.SMEM)


def exchange(blocks, axis):
    return lax.all_to_all(blocks, axis, split_axis=0, concat_axis=0, tiled=True)


def to_all(block, axis):
    return exchange(jnp.broadcast_to(block[None], (lax.axis_size(axis),) + block.shape), axis)


def shards(
    queries,
    root_keys,
    root_values,
    branch_keys,
    branch_values,
    suffix_keys,
    suffix_values,
    new_keys,
    new_values,
    branch_of,
    owner,
    suffix_len,
):
    steps, q_heads, dim = queries.shape[1:]
    heads = root_keys.shape[1]
    group = q_heads // heads
    per_head = steps * group
    rows = heads * per_head
    grp = lax.axis_size("grp")
    sq = lax.axis_size("sq")
    core = lax.axis_size("core")
    grp_place = lax.axis_index("grp")
    seq_place = lax.axis_index("sq") * core + lax.axis_index("core")
    swap = [(0, 1), (1, 0)]

    q_rows = queries[0].reshape(steps, heads, group, dim).transpose(1, 0, 2, 3)
    q_rows = q_rows.reshape(rows, dim)
    peers = to_all(q_rows, "grp")

    matches = branch_of[:, None] == jnp.arange(owner.shape[0])[None, :]
    slot_of = jnp.sum(jnp.where(matches, owner[None, :], 0), axis=1)
    slot_here = lax.dynamic_slice_in_dim(slot_of.reshape(grp, sq * core), seq_place, 1, 1)[:, 0]
    reading = slot_here == grp_place
    group_ids = jnp.arange(grp)
    before = jnp.sum((reading[None, :] & (group_ids[None, :] < group_ids[:, None])), axis=1)
    chosen = reading[None, :] & (before[None, :] == jnp.arange(CAP)[:, None])
    readers = jnp.max(jnp.where(chosen, group_ids[None, :], -1), axis=1).astype(jnp.int32)

    def gather_readers(peers):
        packed = pl.pallas_call(
            select_kernel,
            out_shape=jax.ShapeDtypeStruct((sq, CAP, rows, dim), jnp.bfloat16),
            grid_spec=pltpu.PrefetchScalarGridSpec(
                num_scalar_prefetch=1,
                grid=(CAP,),
                in_specs=[
                    pl.BlockSpec((1, rows, dim), lambda k, idx: (jnp.maximum(idx[k], 0), 0, 0))
                ],
                out_specs=pl.BlockSpec((sq, 1, rows, dim), lambda k, idx: (0, k, 0, 0)),
            ),
            compiler_params=params(),
            name="pick_readers",
        )(readers, peers)
        return exchange(packed, "sq")

    branch_own = jnp.stack([branch_keys[0], branch_values[0]]).transpose(0, 2, 1, 3)
    branch_twin = lax.ppermute(branch_own, "core", swap)
    root_block = jnp.concatenate([root_keys, root_values], axis=0).transpose(1, 0, 2)
    ring = sq // 2
    flip = [(i, (i + ring) % sq) for i in range(sq)]
    up = [(i, i // ring * ring + (i + 1) % ring) for i in range(sq)]
    down = [(b, a) for a, b in up]
    pair = jnp.stack([root_block, lax.ppermute(root_block, "sq", flip)])
    root_blocks = [pair]
    ahead = behind = pair
    for hop in range(ring // 2):
        ahead = lax.ppermute(ahead, "sq", up)
        root_blocks.append(ahead)
        if hop < ring // 2 - 1:
            behind = lax.ppermute(behind, "sq", down)
            root_blocks.append(behind)
        if hop == 0:
            peers, ahead, behind = lax.optimization_barrier((peers, ahead, behind))
            slots = gather_readers(peers)
        if hop == 1:
            slots, ahead, behind = lax.optimization_barrier((slots, ahead, behind))
    peers_twin = lax.ppermute(peers, "core", swap)

    flat = suffix_keys.shape[1] * heads
    local = pl.pallas_call(
        functools.partial(local_kernel, heads),
        out_shape=jax.ShapeDtypeStruct((rows + PAD, dim), jnp.float32),
        in_specs=[smem()] + [vmem()] * 5,
        out_specs=vmem(),
        compiler_params=params(),
        cost_estimate=pl.CostEstimate(
            flops=4 * rows * flat * dim, bytes_accessed=4 * flat * dim, transcendentals=rows * flat
        ),
        name="local_attention",
    )(
        suffix_len,
        q_rows,
        suffix_keys.reshape(flat, dim),
        suffix_values.reshape(flat, dim),
        new_keys.reshape(steps * heads, dim),
        new_values.reshape(steps * heads, dim),
    )

    slots = slots.reshape(sq * CAP, rows, dim)
    block = (2, 1) + branch_own.shape[2:]
    area = sq * CAP * rows * branch_own.shape[2] * core
    parts = pl.pallas_call(
        branch_kernel,
        grid=(heads,),
        out_shape=jax.ShapeDtypeStruct((sq * CAP, rows + PAD, dim), jnp.float32),
        in_specs=[
            pl.BlockSpec((sq * CAP, per_head, dim), lambda j: (0, j, 0)),
            pl.BlockSpec(block, lambda j: (0, j, 0, 0)),
            pl.BlockSpec(block, lambda j: (0, j, 0, 0)),
        ],
        out_specs=pl.BlockSpec((sq * CAP, rows + PAD, dim), lambda j: (0, 0, 0)),
        compiler_params=params(),
        cost_estimate=pl.CostEstimate(
            flops=4 * area * dim, bytes_accessed=4 * 1024 * 1024, transcendentals=area
        ),
        name="branch_attention",
    )(slots, branch_own, branch_twin)
    parts = parts.astype(jnp.float16).reshape(sq, CAP, rows + PAD, dim)
    parts = exchange(parts, "sq").astype(jnp.float32)

    count = len(root_blocks)
    area = 2 * grp * rows * root_keys.shape[0] * sq
    whole = jax.ShapeDtypeStruct((grp, rows + PAD, dim), jnp.float32)
    root_own, root_twin = pl.pallas_call(
        functools.partial(root_kernel, count),
        grid=(heads,),
        out_shape=(whole, whole),
        in_specs=[pl.BlockSpec((grp, per_head, dim), lambda j: (0, j, 0))] * 2
        + [pl.BlockSpec((2, 1) + pair.shape[2:], lambda j: (0, j, 0, 0))] * count,
        out_specs=(pl.BlockSpec(whole.shape, lambda j: (0, 0, 0)),) * 2,
        compiler_params=params(),
        cost_estimate=pl.CostEstimate(
            flops=4 * area * dim, bytes_accessed=5 * 1024 * 1024, transcendentals=area
        ),
        name="root_attention",
    )(peers, peers_twin, *root_blocks)
    root_twin = lax.ppermute(root_twin, "core", swap)

    merged = pl.pallas_call(
        merge_kernel,
        out_shape=whole,
        in_specs=[smem()] + [vmem()] * 3,
        out_specs=vmem(),
        compiler_params=params(),
        name="merge_parts",
    )(readers, parts, root_own, root_twin)
    back = exchange(merged.astype(jnp.float16), "grp").astype(jnp.float32)
    mine = pl.pallas_call(
        final_kernel,
        out_shape=jax.ShapeDtypeStruct((rows, dim), jnp.bfloat16),
        in_specs=[vmem()] * 2,
        out_specs=vmem(),
        compiler_params=params(),
        name="final_merge",
    )(back, local)
    mine = mine.reshape(heads, steps, group, dim).transpose(1, 0, 2, 3)
    return mine.reshape(queries.shape)


def solution(mesh):
    grp, seq = mesh.devices.shape
    fine = Mesh(mesh.devices.reshape(grp, seq // 2, 2), ("grp", "sq", "core"))
    both = ("grp", "sq", "core")
    in_specs = (
        P(both, None, None, None),
        P(both, None, None),
        P(both, None, None),
        P("grp", ("sq", "core"), None, None),
        P("grp", ("sq", "core"), None, None),
        P(both, None, None, None),
        P(both, None, None, None),
        P(both, None, None, None),
        P(both, None, None, None),
        P(),
        P(),
        P(both),
    )
    out_specs = P(both, None, None, None)
    return jax.shard_map(shards, mesh=fine, in_specs=in_specs, out_specs=out_specs, check_vma=False)
```

```python
import functools
import math

import jax
import jax.numpy as jnp
from jax import lax
from jax.experimental import pallas as pl
from jax.experimental.pallas import tpu as pltpu
from jax.sharding import Mesh, PartitionSpec as P

CAP = 2
PAD = 8
LOW = -1e30
EMPHASIS = 30
VMEM_LIMIT = 20 * 1024 * 1024
NT = (((1,), (1,)), ((), ()))


def scores_of(rows, keys):
    raw = lax.dot_general(rows, keys, NT, preferred_element_type=jnp.float32)
    return raw * (1.0 / math.sqrt(keys.shape[-1]))


def times_values(weights, values):
    return jnp.dot(weights.astype(jnp.bfloat16), values, preferred_element_type=jnp.float32)


def head_lse(lse, head, per_head, lanes):
    lse = jnp.broadcast_to(lse, (lse.shape[0], lanes))
    row = lax.broadcasted_iota(jnp.int32, lse.shape, 0)
    col = lax.broadcasted_iota(jnp.int32, lse.shape, 1)
    lse = jnp.where(col == head * per_head + row % per_head, lse, 0.0)
    return jnp.sum(lse.reshape(-1, per_head, lanes), axis=1, keepdims=True)


def tail_rows(pieces):
    shape = pieces[0].shape[:-2] + (PAD, pieces[0].shape[-1])
    row = lax.broadcasted_iota(jnp.int32, shape, len(shape) - 2)
    out = jnp.zeros(shape, jnp.float32)
    for place, piece in enumerate(pieces):
        out = jnp.where(row == place, jnp.broadcast_to(piece, shape), out)
    return out


def split_lse(lse):
    coarse = jnp.round(lse * 0.25) * 4.0
    rest = lse - coarse
    middle = jnp.round(rest * 512.0) * (1.0 / 512.0)
    return coarse, middle, rest - middle


def join_lse(tail):
    return tail[..., 0, :] + tail[..., 1, :] + tail[..., 2, :]


def local_kernel(heads, len_ref, q_ref, k_ref, v_ref, nk_ref, nv_ref, out_ref):
    rows = q_ref.shape[0]
    per_head = rows // heads
    q = q_ref[...]
    far = scores_of(q, k_ref[...])
    row = lax.broadcasted_iota(jnp.int32, far.shape, 0)
    col = lax.broadcasted_iota(jnp.int32, far.shape, 1)
    seen = (col % heads == row // per_head) & (col < len_ref[0] * heads)
    far = jnp.where(seen, far, LOW)
    near = scores_of(q, nk_ref[...])
    row = lax.broadcasted_iota(jnp.int32, near.shape, 0)
    col = lax.broadcasted_iota(jnp.int32, near.shape, 1)
    steps = near.shape[1] // heads
    step = (row % per_head) // (per_head // steps)
    seen = (col % heads == row // per_head) & (col // heads <= step)
    near = jnp.where(seen, near, LOW)
    high = jnp.maximum(
        jnp.max(far, axis=1, keepdims=True), jnp.max(near, axis=1, keepdims=True)
    )
    far = jnp.exp(far - high)
    near = jnp.exp(near - high)
    den = jnp.sum(far, axis=1, keepdims=True) + jnp.sum(near, axis=1, keepdims=True)
    num = times_values(far, v_ref[...]) + times_values(near, nv_ref[...])
    out_ref[:rows, :] = num / den
    lse = jnp.broadcast_to(high + jnp.log(den), (rows, rows))
    row = lax.broadcasted_iota(jnp.int32, (rows, rows), 0)
    col = lax.broadcasted_iota(jnp.int32, (rows, rows), 1)
    flat = jnp.sum(jnp.where(row == col, lse, 0.0), axis=0, keepdims=True)
    out_ref[rows:, :] = jnp.broadcast_to(flat, (PAD, rows))


def select_kernel(idx_ref, peer_ref, out_ref):
    out_ref[...] = jnp.broadcast_to(peer_ref[...][None], out_ref.shape)


def branch_kernel(q_ref, *refs):
    out_ref = refs[-1]
    blocks = list(zip(refs[:-1:2], refs[1:-1:2]))
    slots, lanes, dim = q_ref.shape
    heads = refs[0].shape[0]
    per_head = lanes // heads
    tail = jnp.zeros((slots, 1, lanes), jnp.float32)
    for head in range(heads):
        place = slice(head * per_head, (head + 1) * per_head)
        q = q_ref[:, place, :].reshape(slots * per_head, dim)
        found = []
        for k_ref, v_ref in blocks:
            scores = scores_of(q, k_ref[head])
            high = jnp.max(scores, axis=1, keepdims=True)
            weights = jnp.exp(scores - high)
            den = jnp.sum(weights, axis=1, keepdims=True)
            found.append((high, den, times_values(weights, v_ref[head])))
        high = functools.reduce(jnp.maximum, [f[0] for f in found])
        factors = [jnp.exp(f[0] - high) for f in found]
        den = sum(factor * f[1] for factor, f in zip(factors, found))
        num = sum(f[2] * (factor / den) for factor, f in zip(factors, found))
        out_ref[:, place, :] = num.reshape(slots, per_head, dim)
        tail = tail + head_lse(high + jnp.log(den), head, per_head, lanes)
    out_ref[:, lanes:, :] = tail_rows(split_lse(tail))


def root_kernel(q_ref, own_ref, twin_ref, out_ref):
    requests, lanes, dim = q_ref.shape
    count, heads = own_ref.shape[:2]
    per_head = lanes // heads
    half = own_ref.shape[2] // 2
    tail = jnp.zeros((requests, 1, lanes), jnp.float32)
    for head in range(heads):
        place = slice(head * per_head, (head + 1) * per_head)
        q = q_ref[:, place, :].reshape(requests * per_head, dim)
        blocks = [r[:, head, :, :] for r in (own_ref, twin_ref)]
        keys = [block[:, :half, :].reshape(count * half, dim) for block in blocks]
        values = [block[:, half:, :].reshape(count * half, dim) for block in blocks]
        scores = [scores_of(q, k) for k in keys]
        high = functools.reduce(
            jnp.maximum, [jnp.max(s, axis=1, keepdims=True) for s in scores]
        )
        weights = [jnp.exp(s - high) for s in scores]
        den = sum(jnp.sum(w, axis=1, keepdims=True) for w in weights)
        num = sum(times_values(w, v) for w, v in zip(weights, values)) / den
        out_ref[:, place, :] = num.reshape(requests, per_head, dim)
        tail = tail + head_lse(high + jnp.log(den), head, per_head, lanes)
    out_ref[:, lanes:, :] = tail_rows(split_lse(tail))


def columns(table):
    lanes = table.shape[1]
    rest = jnp.zeros((lanes - table.shape[0], lanes), jnp.float32)
    return jnp.concatenate([table, rest], axis=0).T


def merge_kernel(idx_ref, part_ref, root_ref, out_ref):
    sources, cap, _, lanes = part_ref.shape
    out_ref[...] = root_ref[...]
    for k in range(cap):
        reader = idx_ref[k]

        @pl.when(reader >= 0)
        def _():
            lse = join_lse(part_ref[:, k, lanes:, :])
            near = join_lse(out_ref[reader, lanes:, :])[None]
            high = jnp.maximum(jnp.max(lse, axis=0, keepdims=True), near)
            factor = jnp.exp(lse - high)
            near = jnp.exp(near - high)
            total = jnp.sum(factor, axis=0, keepdims=True) + near
            table = columns(jnp.concatenate([factor / total, near / total], axis=0))
            out = out_ref[reader, :lanes, :] * table[:, sources : sources + 1]
            for source in range(sources):
                out = out + part_ref[source, k, :lanes, :] * table[:, source : source + 1]
            out_ref[reader, :lanes, :] = out
            out_ref[reader, lanes:, :] = tail_rows(split_lse(high + jnp.log(total)))


def final_kernel(part_ref, local_ref, out_ref):
    groups, _, lanes = part_ref.shape
    lse = join_lse(part_ref[:, lanes:, :])
    near = local_ref[lanes : lanes + 1, :]
    high = jnp.maximum(jnp.max(lse, axis=0, keepdims=True), near)
    factor = jnp.exp(lse - high)
    near = jnp.exp(near - high)
    total = jnp.sum(factor, axis=0, keepdims=True) + near
    table = columns(jnp.concatenate([factor / total, near / total], axis=0))
    out = local_ref[:lanes, :] * table[:, groups : groups + 1]
    for source in range(groups):
        out = out + part_ref[source, :lanes, :] * table[:, source : source + 1]
    out_ref[...] = out.astype(out_ref.dtype)


def params():
    return pltpu.CompilerParams(vmem_limit_bytes=VMEM_LIMIT)


def estimate(area, dim):
    return pl.CostEstimate(
        flops=EMPHASIS * 4 * area * dim, bytes_accessed=6 * 1024 * 1024, transcendentals=area
    )


def vmem():
    return pl.BlockSpec(memory_space=pltpu.VMEM)


def smem():
    return pl.BlockSpec(memory_space=pltpu.SMEM)


def exchange(blocks, axis):
    return lax.all_to_all(blocks, axis, split_axis=0, concat_axis=0, tiled=True)


def to_all(block, axis):
    return exchange(jnp.broadcast_to(block[None], (lax.axis_size(axis),) + block.shape), axis)


def shards(
    queries,
    root_keys,
    root_values,
    branch_keys,
    branch_values,
    suffix_keys,
    suffix_values,
    new_keys,
    new_values,
    branch_of,
    owner,
    suffix_len,
):
    steps, q_heads, dim = queries.shape[1:]
    heads = root_keys.shape[1]
    group = q_heads // heads
    per_head = steps * group
    rows = heads * per_head
    grp = lax.axis_size("grp")
    ring = lax.axis_size("z")
    core = lax.axis_size("core")
    spots = lax.axis_size("xhi") * ring * core
    grp_place = lax.axis_index("grp")
    seq_place = (lax.axis_index("xhi") * ring + lax.axis_index("z")) * core + lax.axis_index("core")
    swap = [(0, 1), (1, 0)]

    q_rows = queries[0].reshape(steps, heads, group, dim).transpose(1, 0, 2, 3)
    q_rows = q_rows.reshape(rows, dim)
    peers = to_all(q_rows, "grp")

    matches = branch_of[:, None] == jnp.arange(owner.shape[0])[None, :]
    slot_of = jnp.sum(jnp.where(matches, owner[None, :], 0), axis=1)
    slot_here = lax.dynamic_slice_in_dim(slot_of.reshape(grp, spots), seq_place, 1, 1)[:, 0]
    reading = slot_here == grp_place
    group_ids = jnp.arange(grp)
    before = jnp.sum((reading[None, :] & (group_ids[None, :] < group_ids[:, None])), axis=1)
    chosen = reading[None, :] & (before[None, :] == jnp.arange(CAP)[:, None])
    readers = jnp.max(jnp.where(chosen, group_ids[None, :], -1), axis=1).astype(jnp.int32)

    area = ring * CAP * rows * branch_keys.shape[1] * 4

    def gather_readers(peers):
        packed = pl.pallas_call(
            select_kernel,
            out_shape=jax.ShapeDtypeStruct((ring, CAP, rows, dim), jnp.bfloat16),
            grid_spec=pltpu.PrefetchScalarGridSpec(
                num_scalar_prefetch=1,
                grid=(CAP,),
                in_specs=[
                    pl.BlockSpec((1, rows, dim), lambda k, idx: (jnp.maximum(idx[k], 0), 0, 0))
                ],
                out_specs=pl.BlockSpec((ring, 1, rows, dim), lambda k, idx: (0, k, 0, 0)),
            ),
            compiler_params=params(),
            cost_estimate=estimate(area, dim),
            name="pick_readers",
        )(readers, peers)
        return exchange(packed, "z")

    keys_own = branch_keys[0].transpose(1, 0, 2)
    values_own = branch_values[0].transpose(1, 0, 2)
    root_block = jnp.concatenate([root_keys, root_values], axis=0).transpose(1, 0, 2)
    root_far = lax.ppermute(root_block, "xhi", swap)
    root_far, keys_own, values_own = lax.optimization_barrier((root_far, keys_own, values_own))
    root_blocks = lax.all_gather(jnp.stack([root_block, root_far]), "z", axis=0, tiled=True)
    keys_far = lax.ppermute(keys_own, "xhi", swap)
    values_far = lax.ppermute(values_own, "xhi", swap)
    slots = gather_readers(peers)
    branch_blocks = [
        keys_own,
        values_own,
        lax.ppermute(keys_own, "core", swap),
        lax.ppermute(values_own, "core", swap),
        keys_far,
        values_far,
        lax.ppermute(keys_far, "core", swap),
        lax.ppermute(values_far, "core", swap),
    ]

    flat = suffix_keys.shape[1] * heads
    local = pl.pallas_call(
        functools.partial(local_kernel, heads),
        out_shape=jax.ShapeDtypeStruct((rows + PAD, dim), jnp.float32),
        in_specs=[smem()] + [vmem()] * 5,
        out_specs=vmem(),
        compiler_params=params(),
        cost_estimate=pl.CostEstimate(
            flops=4 * rows * flat * dim, bytes_accessed=4 * flat * dim, transcendentals=rows * flat
        ),
        name="local_attention",
    )(
        suffix_len,
        q_rows,
        suffix_keys.reshape(flat, dim),
        suffix_values.reshape(flat, dim),
        new_keys.reshape(steps * heads, dim),
        new_values.reshape(steps * heads, dim),
    )

    slots = slots.reshape(ring * CAP, rows, dim)
    area = ring * CAP * rows * keys_own.shape[1] * 4
    parts = pl.pallas_call(
        branch_kernel,
        out_shape=jax.ShapeDtypeStruct((ring * CAP, rows + PAD, dim), jnp.float32),
        in_specs=[vmem()] * (1 + len(branch_blocks)),
        out_specs=vmem(),
        compiler_params=params(),
        cost_estimate=estimate(area, dim),
        name="branch_attention",
    )(slots, *branch_blocks)
    parts = parts.astype(jnp.float16).reshape(ring, CAP, rows + PAD, dim)
    root_blocks, peers, _ = lax.optimization_barrier((root_blocks, peers, parts))
    root_twin = lax.ppermute(root_blocks, "core", swap)
    parts = exchange(parts, "z")

    area = grp * rows * root_keys.shape[0] * 4 * ring
    whole = jax.ShapeDtypeStruct((grp, rows + PAD, dim), jnp.float32)
    root = pl.pallas_call(
        root_kernel,
        out_shape=whole,
        in_specs=[vmem()] * 3,
        out_specs=vmem(),
        compiler_params=params(),
        cost_estimate=estimate(area, dim),
        name="root_attention",
    )(peers, root_blocks, root_twin)

    parts, root = lax.optimization_barrier((parts, root))
    parts = parts.astype(jnp.float32)
    merged = pl.pallas_call(
        merge_kernel,
        out_shape=whole,
        in_specs=[smem()] + [vmem()] * 2,
        out_specs=vmem(),
        compiler_params=params(),
        name="merge_parts",
    )(readers, parts, root)
    back = exchange(merged.astype(jnp.float16), "grp").astype(jnp.float32)
    mine = pl.pallas_call(
        final_kernel,
        out_shape=jax.ShapeDtypeStruct((rows, dim), jnp.bfloat16),
        in_specs=[vmem()] * 2,
        out_specs=vmem(),
        compiler_params=params(),
        name="final_merge",
    )(back, local)
    mine = mine.reshape(heads, steps, group, dim).transpose(1, 0, 2, 3)
    return mine.reshape(queries.shape)


def solution(mesh):
    grp, seq = mesh.devices.shape
    fine = Mesh(mesh.devices.reshape(grp, 2, seq // 4, 2), ("grp", "xhi", "z", "core"))
    seq = ("xhi", "z", "core")
    both = ("grp",) + seq
    in_specs = (
        P(both, None, None, None),
        P(both, None, None),
        P(both, None, None),
        P("grp", seq, None, None),
        P("grp", seq, None, None),
        P(both, None, None, None),
        P(both, None, None, None),
        P(both, None, None, None),
        P(both, None, None, None),
        P(),
        P(),
        P(both),
    )
    out_specs = P(both, None, None, None)
    return jax.shard_map(shards, mesh=fine, in_specs=in_specs, out_specs=out_specs, check_vma=False)
```

```python
import functools
import math

import jax
import jax.numpy as jnp
from jax import lax
from jax.experimental import pallas as pl
from jax.experimental.pallas import tpu as pltpu
from jax.sharding import Mesh, PartitionSpec as P

CAP = 2
PAD = 8
LOW = -1e30
EMPHASIS = 30
NT = (((1,), (1,)), ((), ()))


def scores_of(rows, keys):
    raw = lax.dot_general(rows, keys, NT, preferred_element_type=jnp.float32)
    return raw * (1.0 / math.sqrt(keys.shape[-1]))


def times_values(weights, values):
    return jnp.dot(weights.astype(jnp.bfloat16), values, preferred_element_type=jnp.float32)


def head_lse(lse, head, per_head, lanes):
    lse = jnp.broadcast_to(lse, (lse.shape[0], lanes))
    row = lax.broadcasted_iota(jnp.int32, lse.shape, 0)
    col = lax.broadcasted_iota(jnp.int32, lse.shape, 1)
    lse = jnp.where(col == head * per_head + row % per_head, lse, 0.0)
    return jnp.sum(lse.reshape(-1, per_head, lanes), axis=1, keepdims=True)


def tail_rows(pieces):
    shape = pieces[0].shape[:-2] + (PAD, pieces[0].shape[-1])
    row = lax.broadcasted_iota(jnp.int32, shape, len(shape) - 2)
    out = jnp.zeros(shape, jnp.float32)
    for place, piece in enumerate(pieces):
        out = jnp.where(row == place, jnp.broadcast_to(piece, shape), out)
    return out


def split_lse(lse):
    coarse = jnp.round(lse * 0.25) * 4.0
    rest = lse - coarse
    middle = jnp.round(rest * 512.0) * (1.0 / 512.0)
    return coarse, middle, rest - middle


def join_lse(tail):
    return tail[..., 0, :] + tail[..., 1, :] + tail[..., 2, :]


def local_kernel(heads, len_ref, q_ref, k_ref, v_ref, nk_ref, nv_ref, out_ref):
    rows = q_ref.shape[0]
    per_head = rows // heads
    q = q_ref[...]
    far = scores_of(q, k_ref[...])
    row = lax.broadcasted_iota(jnp.int32, far.shape, 0)
    col = lax.broadcasted_iota(jnp.int32, far.shape, 1)
    seen = (col % heads == row // per_head) & (col < len_ref[0] * heads)
    far = jnp.where(seen, far, LOW)
    near = scores_of(q, nk_ref[...])
    row = lax.broadcasted_iota(jnp.int32, near.shape, 0)
    col = lax.broadcasted_iota(jnp.int32, near.shape, 1)
    steps = near.shape[1] // heads
    step = (row % per_head) // (per_head // steps)
    seen = (col % heads == row // per_head) & (col // heads <= step)
    near = jnp.where(seen, near, LOW)
    high = jnp.maximum(
        jnp.max(far, axis=1, keepdims=True), jnp.max(near, axis=1, keepdims=True)
    )
    far = jnp.exp(far - high)
    near = jnp.exp(near - high)
    den = jnp.sum(far, axis=1, keepdims=True) + jnp.sum(near, axis=1, keepdims=True)
    num = times_values(far, v_ref[...]) + times_values(near, nv_ref[...])
    out_ref[:rows, :] = num / den
    lse = jnp.broadcast_to(high + jnp.log(den), (rows, rows))
    row = lax.broadcasted_iota(jnp.int32, (rows, rows), 0)
    col = lax.broadcasted_iota(jnp.int32, (rows, rows), 1)
    flat = jnp.sum(jnp.where(row == col, lse, 0.0), axis=0, keepdims=True)
    out_ref[rows:, :] = jnp.broadcast_to(flat, (PAD, rows))


def select_kernel(idx_ref, peer_ref, out_ref):
    out_ref[...] = jnp.broadcast_to(peer_ref[...][None], out_ref.shape)


def branch_kernel(count, q_ref, *refs):
    sources, out_ref, held, sems = refs[:count], refs[count], refs[count + 1], refs[count + 2]
    slots, lanes, dim = q_ref.shape
    heads = sources[0].shape[0]
    per_head = lanes // heads

    def copies(head):
        return [
            pltpu.make_async_copy(ref.at[head], held.at[place, head], sems.at[place, head])
            for place, ref in enumerate(sources)
        ]

    for head in range(heads):
        for copy in copies(head):
            copy.start()
    tail = jnp.zeros((slots, 1, lanes), jnp.float32)
    for head in range(heads):
        for copy in copies(head):
            copy.wait()
        place = slice(head * per_head, (head + 1) * per_head)
        q = q_ref[:, place, :].reshape(slots * per_head, dim)
        found = []
        for block in range(0, count, 2):
            scores = scores_of(q, held[block, head])
            high = jnp.max(scores, axis=1, keepdims=True)
            weights = jnp.exp(scores - high)
            den = jnp.sum(weights, axis=1, keepdims=True)
            found.append((high, den, times_values(weights, held[block + 1, head])))
        high = functools.reduce(jnp.maximum, [f[0] for f in found])
        factors = [jnp.exp(f[0] - high) for f in found]
        den = sum(factor * f[1] for factor, f in zip(factors, found))
        num = sum(f[2] * (factor / den) for factor, f in zip(factors, found))
        out_ref[:, place, :] = num.reshape(slots, per_head, dim)
        tail = tail + head_lse(high + jnp.log(den), head, per_head, lanes)
    out_ref[:, lanes:, :] = tail_rows(split_lse(tail))


def root_kernel(count, q_ref, q_twin_ref, *refs):
    sources, out_refs = refs[:count], refs[count : count + 2]
    held, sems = refs[count + 2 :]
    copies = [
        pltpu.make_async_copy(ref, held.at[place], sems.at[place])
        for place, ref in enumerate(sources)
    ]
    for copy in copies:
        copy.start()
    for copy in copies:
        copy.wait()
    requests, lanes, dim = q_ref.shape
    pairs, heads, half = held.shape[1], held.shape[2], held.shape[3] // 2
    per_head = lanes // heads
    span = count * pairs * half
    tails = [jnp.zeros((requests, 1, lanes), jnp.float32) for _ in out_refs]
    for head in range(heads):
        place = slice(head * per_head, (head + 1) * per_head)
        keys = held[:, :, head, :half, :].reshape(span, dim)
        values = held[:, :, head, half:, :].reshape(span, dim)
        for which, (rows_ref, out_ref) in enumerate(zip((q_ref, q_twin_ref), out_refs)):
            q = rows_ref[:, place, :].reshape(requests * per_head, dim)
            scores = scores_of(q, keys)
            high = jnp.max(scores, axis=1, keepdims=True)
            weights = jnp.exp(scores - high)
            den = jnp.sum(weights, axis=1, keepdims=True)
            num = times_values(weights, values) / den
            out_ref[:, place, :] = num.reshape(requests, per_head, dim)
            tails[which] = tails[which] + head_lse(high + jnp.log(den), head, per_head, lanes)
    for out_ref, tail in zip(out_refs, tails):
        out_ref[:, lanes:, :] = tail_rows(split_lse(tail))


def columns(table):
    lanes = table.shape[1]
    rest = jnp.zeros((lanes - table.shape[0], lanes), jnp.float32)
    return jnp.concatenate([table, rest], axis=0).T


def merge_kernel(idx_ref, part_ref, own_ref, twin_ref, out_ref):
    sources, cap, _, lanes = part_ref.shape
    groups = own_ref.shape[0]
    lse_a = join_lse(own_ref[:, lanes:, :])
    lse_b = join_lse(twin_ref[:, lanes:, :])
    high = jnp.maximum(lse_a, lse_b)
    factor_a = jnp.exp(lse_a - high)
    factor_b = jnp.exp(lse_b - high)
    total = factor_a + factor_b
    table = columns(jnp.concatenate([factor_a / total, factor_b / total], axis=0))
    pieces = split_lse(high + jnp.log(total))
    for r in range(groups):
        out_ref[r, :lanes, :] = (
            own_ref[r, :lanes, :] * table[:, r : r + 1]
            + twin_ref[r, :lanes, :] * table[:, groups + r : groups + r + 1]
        )
        out_ref[r, lanes:, :] = tail_rows([piece[r : r + 1] for piece in pieces])
    for k in range(cap):
        reader = idx_ref[k]

        @pl.when(reader >= 0)
        def _():
            lse = join_lse(part_ref[:, k, lanes:, :])
            near = join_lse(out_ref[reader, lanes:, :])[None]
            high = jnp.maximum(jnp.max(lse, axis=0, keepdims=True), near)
            factor = jnp.exp(lse - high)
            near = jnp.exp(near - high)
            total = jnp.sum(factor, axis=0, keepdims=True) + near
            table = columns(jnp.concatenate([factor / total, near / total], axis=0))
            out = out_ref[reader, :lanes, :] * table[:, sources : sources + 1]
            for source in range(sources):
                out = out + part_ref[source, k, :lanes, :] * table[:, source : source + 1]
            out_ref[reader, :lanes, :] = out
            out_ref[reader, lanes:, :] = tail_rows(split_lse(high + jnp.log(total)))


def final_kernel(part_ref, local_ref, out_ref):
    groups, _, lanes = part_ref.shape
    lse = join_lse(part_ref[:, lanes:, :])
    near = local_ref[lanes : lanes + 1, :]
    high = jnp.maximum(jnp.max(lse, axis=0, keepdims=True), near)
    factor = jnp.exp(lse - high)
    near = jnp.exp(near - high)
    total = jnp.sum(factor, axis=0, keepdims=True) + near
    table = columns(jnp.concatenate([factor / total, near / total], axis=0))
    out = local_ref[:lanes, :] * table[:, groups : groups + 1]
    for source in range(groups):
        out = out + part_ref[source, :lanes, :] * table[:, source : source + 1]
    out_ref[...] = out.astype(out_ref.dtype)


def params(megabytes=48):
    return pltpu.CompilerParams(vmem_limit_bytes=megabytes * 1024 * 1024)


def estimate(area, dim):
    return pl.CostEstimate(
        flops=EMPHASIS * 4 * area * dim, bytes_accessed=6 * 1024 * 1024, transcendentals=area
    )


def vmem():
    return pl.BlockSpec(memory_space=pltpu.VMEM)


def hbm():
    return pl.BlockSpec(memory_space=pltpu.HBM)


def smem():
    return pl.BlockSpec(memory_space=pltpu.SMEM)


def exchange(blocks, axis):
    return lax.all_to_all(blocks, axis, split_axis=0, concat_axis=0, tiled=True)


def to_all(block, axis):
    return exchange(jnp.broadcast_to(block[None], (lax.axis_size(axis),) + block.shape), axis)


def shards(
    queries,
    root_keys,
    root_values,
    branch_keys,
    branch_values,
    suffix_keys,
    suffix_values,
    new_keys,
    new_values,
    branch_of,
    owner,
    suffix_len,
):
    steps, q_heads, dim = queries.shape[1:]
    heads = root_keys.shape[1]
    group = q_heads // heads
    per_head = steps * group
    rows = heads * per_head
    grp = lax.axis_size("grp")
    ring = lax.axis_size("z")
    core = lax.axis_size("core")
    spots = lax.axis_size("xhi") * ring * core
    grp_place = lax.axis_index("grp")
    seq_place = (lax.axis_index("xhi") * ring + lax.axis_index("z")) * core + lax.axis_index("core")
    swap = [(0, 1), (1, 0)]

    q_rows = queries[0].reshape(steps, heads, group, dim).transpose(1, 0, 2, 3)
    q_rows = q_rows.reshape(rows, dim)
    peers = to_all(q_rows, "grp")

    matches = branch_of[:, None] == jnp.arange(owner.shape[0])[None, :]
    slot_of = jnp.sum(jnp.where(matches, owner[None, :], 0), axis=1)
    slot_here = lax.dynamic_slice_in_dim(slot_of.reshape(grp, spots), seq_place, 1, 1)[:, 0]
    reading = slot_here == grp_place
    group_ids = jnp.arange(grp)
    before = jnp.sum((reading[None, :] & (group_ids[None, :] < group_ids[:, None])), axis=1)
    chosen = reading[None, :] & (before[None, :] == jnp.arange(CAP)[:, None])
    readers = jnp.max(jnp.where(chosen, group_ids[None, :], -1), axis=1).astype(jnp.int32)

    area = ring * CAP * rows * branch_keys.shape[1] * 4

    def gather_readers(peers):
        packed = pl.pallas_call(
            select_kernel,
            out_shape=jax.ShapeDtypeStruct((ring, CAP, rows, dim), jnp.bfloat16),
            grid_spec=pltpu.PrefetchScalarGridSpec(
                num_scalar_prefetch=1,
                grid=(CAP,),
                in_specs=[
                    pl.BlockSpec((1, rows, dim), lambda k, idx: (jnp.maximum(idx[k], 0), 0, 0))
                ],
                out_specs=pl.BlockSpec((ring, 1, rows, dim), lambda k, idx: (0, k, 0, 0)),
            ),
            compiler_params=params(),
            cost_estimate=estimate(area, dim),
            name="pick_readers",
        )(readers, peers)
        return exchange(packed, "z")

    keys_own = branch_keys[0].transpose(1, 0, 2)
    values_own = branch_values[0].transpose(1, 0, 2)
    root_block = jnp.concatenate([root_keys, root_values], axis=0).transpose(1, 0, 2)
    root_far = lax.ppermute(root_block, "xhi", swap)
    up = [(i, (i + 1) % ring) for i in range(ring)]
    down = [(b, a) for a, b in up]
    pair = jnp.stack([root_block, root_far])
    root_blocks = [pair]

    def hop(ahead, behind):
        ahead = lax.ppermute(ahead, "z", up)
        root_blocks.append(ahead)
        if len(root_blocks) < ring:
            behind = lax.ppermute(behind, "z", down)
            root_blocks.append(behind)
        return ahead, behind

    pair, keys_own, values_own = lax.optimization_barrier((pair, keys_own, values_own))
    ahead, behind = hop(pair, pair)
    keys_far = lax.ppermute(keys_own, "xhi", swap)
    values_far = lax.ppermute(values_own, "xhi", swap)
    peers, ahead, behind = lax.optimization_barrier((peers, ahead, behind))
    slots = gather_readers(peers)
    while len(root_blocks) < ring:
        ahead, behind = hop(ahead, behind)
    branch_blocks = [
        keys_own,
        values_own,
        lax.ppermute(keys_own, "core", swap),
        lax.ppermute(values_own, "core", swap),
        keys_far,
        values_far,
        lax.ppermute(keys_far, "core", swap),
        lax.ppermute(values_far, "core", swap),
    ]
    peers_twin = lax.ppermute(peers, "core", swap)

    flat = suffix_keys.shape[1] * heads
    local = pl.pallas_call(
        functools.partial(local_kernel, heads),
        out_shape=jax.ShapeDtypeStruct((rows + PAD, dim), jnp.float32),
        in_specs=[smem()] + [vmem()] * 5,
        out_specs=vmem(),
        compiler_params=params(),
        cost_estimate=pl.CostEstimate(
            flops=4 * rows * flat * dim, bytes_accessed=4 * flat * dim, transcendentals=rows * flat
        ),
        name="local_attention",
    )(
        suffix_len,
        q_rows,
        suffix_keys.reshape(flat, dim),
        suffix_values.reshape(flat, dim),
        new_keys.reshape(steps * heads, dim),
        new_values.reshape(steps * heads, dim),
    )

    slots = slots.reshape(ring * CAP, rows, dim)
    area = ring * CAP * rows * branch_keys.shape[1] * 4
    count = len(branch_blocks)
    parts = pl.pallas_call(
        functools.partial(branch_kernel, count),
        out_shape=jax.ShapeDtypeStruct((ring * CAP, rows + PAD, dim), jnp.float32),
        in_specs=[vmem()] + [hbm()] * count,
        out_specs=vmem(),
        scratch_shapes=[
            pltpu.VMEM((count,) + keys_own.shape, jnp.bfloat16),
            pltpu.SemaphoreType.DMA((count, heads)),
        ],
        compiler_params=params(58),
        cost_estimate=estimate(area, dim),
        name="branch_attention",
    )(slots, *branch_blocks)
    parts = parts.astype(jnp.float16).reshape(ring, CAP, rows + PAD, dim)
    peers, _ = lax.optimization_barrier((peers, parts))
    parts = exchange(parts, "z")

    whole = jax.ShapeDtypeStruct((grp, rows + PAD, dim), jnp.float32)
    root_own, root_twin = pl.pallas_call(
        functools.partial(root_kernel, ring),
        out_shape=(whole, whole),
        in_specs=[vmem()] * 2 + [hbm()] * ring,
        out_specs=(vmem(), vmem()),
        scratch_shapes=[
            pltpu.VMEM((ring,) + pair.shape, jnp.bfloat16),
            pltpu.SemaphoreType.DMA((ring,)),
        ],
        compiler_params=params(58),
        cost_estimate=estimate(area, dim),
        name="root_attention",
    )(peers, peers_twin, *root_blocks)
    root_twin = lax.ppermute(root_twin.astype(jnp.float16), "core", swap).astype(jnp.float32)
    parts, root_own, root_twin = lax.optimization_barrier((parts, root_own, root_twin))
    parts = parts.astype(jnp.float32)
    merged = pl.pallas_call(
        merge_kernel,
        out_shape=whole,
        in_specs=[smem()] + [vmem()] * 3,
        out_specs=vmem(),
        compiler_params=params(),
        name="merge_parts",
    )(readers, parts, root_own, root_twin)
    back = exchange(merged.astype(jnp.float16), "grp").astype(jnp.float32)
    mine = pl.pallas_call(
        final_kernel,
        out_shape=jax.ShapeDtypeStruct((rows, dim), jnp.bfloat16),
        in_specs=[vmem()] * 2,
        out_specs=vmem(),
        compiler_params=params(),
        name="final_merge",
    )(back, local)
    mine = mine.reshape(heads, steps, group, dim).transpose(1, 0, 2, 3)
    return mine.reshape(queries.shape)


def solution(mesh):
    grp, seq = mesh.devices.shape
    fine = Mesh(mesh.devices.reshape(grp, 2, seq // 4, 2), ("grp", "xhi", "z", "core"))
    seq = ("xhi", "z", "core")
    both = ("grp",) + seq
    in_specs = (
        P(both, None, None, None),
        P(both, None, None),
        P(both, None, None),
        P("grp", seq, None, None),
        P("grp", seq, None, None),
        P(both, None, None, None),
        P(both, None, None, None),
        P(both, None, None, None),
        P(both, None, None, None),
        P(),
        P(),
        P(both),
    )
    out_specs = P(both, None, None, None)
    return jax.shard_map(shards, mesh=fine, in_specs=in_specs, out_specs=out_specs, check_vma=False)
```

```python
import functools
import math

import jax
import jax.numpy as jnp
from jax import lax
from jax.experimental import pallas as pl
from jax.experimental.pallas import tpu as pltpu
from jax.sharding import Mesh, PartitionSpec as P

CAP = 2
PAD = 8
LOW = -1e30
PARTS = 4
EMPHASIS = 30
NT = (((1,), (1,)), ((), ()))


def scores_of(rows, keys):
    raw = lax.dot_general(rows, keys, NT, preferred_element_type=jnp.float32)
    return raw * (1.0 / math.sqrt(keys.shape[-1]))


def times_values(weights, values):
    return jnp.dot(weights.astype(jnp.bfloat16), values, preferred_element_type=jnp.float32)


def head_lse(lse, head, per_head, lanes):
    lse = jnp.broadcast_to(lse, (lse.shape[0], lanes))
    row = lax.broadcasted_iota(jnp.int32, lse.shape, 0)
    col = lax.broadcasted_iota(jnp.int32, lse.shape, 1)
    lse = jnp.where(col == head * per_head + row % per_head, lse, 0.0)
    return jnp.sum(lse.reshape(-1, per_head, lanes), axis=1, keepdims=True)


def tail_rows(pieces):
    shape = pieces[0].shape[:-2] + (PAD, pieces[0].shape[-1])
    row = lax.broadcasted_iota(jnp.int32, shape, len(shape) - 2)
    out = jnp.zeros(shape, jnp.float32)
    for place, piece in enumerate(pieces):
        out = jnp.where(row == place, jnp.broadcast_to(piece, shape), out)
    return out


def split_lse(lse):
    coarse = jnp.round(lse * 0.25) * 4.0
    rest = lse - coarse
    middle = jnp.round(rest * 512.0) * (1.0 / 512.0)
    return coarse, middle, rest - middle


def join_lse(tail):
    return tail[..., 0, :] + tail[..., 1, :] + tail[..., 2, :]


def local_kernel(heads, len_ref, q_ref, k_ref, v_ref, nk_ref, nv_ref, out_ref):
    rows = q_ref.shape[0]
    per_head = rows // heads
    q = q_ref[...]
    far = scores_of(q, k_ref[...])
    row = lax.broadcasted_iota(jnp.int32, far.shape, 0)
    col = lax.broadcasted_iota(jnp.int32, far.shape, 1)
    seen = (col % heads == row // per_head) & (col < len_ref[0] * heads)
    far = jnp.where(seen, far, LOW)
    near = scores_of(q, nk_ref[...])
    row = lax.broadcasted_iota(jnp.int32, near.shape, 0)
    col = lax.broadcasted_iota(jnp.int32, near.shape, 1)
    steps = near.shape[1] // heads
    step = (row % per_head) // (per_head // steps)
    seen = (col % heads == row // per_head) & (col // heads <= step)
    near = jnp.where(seen, near, LOW)
    high = jnp.maximum(
        jnp.max(far, axis=1, keepdims=True), jnp.max(near, axis=1, keepdims=True)
    )
    far = jnp.exp(far - high)
    near = jnp.exp(near - high)
    den = jnp.sum(far, axis=1, keepdims=True) + jnp.sum(near, axis=1, keepdims=True)
    num = times_values(far, v_ref[...]) + times_values(near, nv_ref[...])
    out_ref[:rows, :] = num / den
    lse = jnp.broadcast_to(high + jnp.log(den), (rows, rows))
    row = lax.broadcasted_iota(jnp.int32, (rows, rows), 0)
    col = lax.broadcasted_iota(jnp.int32, (rows, rows), 1)
    flat = jnp.sum(jnp.where(row == col, lse, 0.0), axis=0, keepdims=True)
    out_ref[rows:, :] = jnp.broadcast_to(flat, (PAD, rows))


def select_kernel(idx_ref, peer_ref, out_ref):
    out_ref[...] = jnp.broadcast_to(peer_ref[...][None], out_ref.shape)


def staged(heads, per_head, queries, results, q_sems, out_sems, feeds, feed_sem):
    parts = out_sems.shape[1] - 1
    group = heads // parts
    reads = [
        [
            pltpu.make_async_copy(source(part), target(part), feed_sem(place, part))
            for place, (source, target) in enumerate(feeds)
        ]
        for part in range(parts)
    ]
    q_copies = [
        pltpu.make_async_copy(ref, held, q_sems.at[place])
        for place, (ref, held) in enumerate(queries)
    ]
    for copy in q_copies:
        copy.start()
    for copies in reads:
        for copy in copies:
            copy.start()
    for copy in q_copies:
        copy.wait()
    span = group * per_head
    pieces = [pl.ds(part * span, span) for part in range(parts)]
    pieces.append(pl.ds(heads * per_head, PAD))
    writes = [
        [
            pltpu.make_async_copy(
                held.at[:, piece, :], ref.at[:, piece, :], out_sems.at[place, part]
            )
            for place, (ref, held) in enumerate(results)
        ]
        for part, piece in enumerate(pieces)
    ]

    def enter(head):
        if head % group == 0:
            for copy in reads[head // group]:
                copy.wait()

    def leave(head):
        if (head + 1) % group == 0:
            for copy in writes[head // group]:
                copy.start()

    def finish():
        for copy in writes[-1]:
            copy.start()
        for copies in writes:
            for copy in copies:
                copy.wait()

    return enter, leave, finish


def branch_kernel(count, q_ref, *refs):
    sources, out_ref = refs[:count], refs[count]
    held, q_held, out_held, sems, q_sems, out_sems = refs[count + 1 :]
    slots, lanes, dim = q_ref.shape
    heads = sources[0].shape[0]
    per_head = lanes // heads
    group = heads // sems.shape[1]

    def feed(place, ref):
        def some(part):
            return pl.ds(part * group, group)

        return lambda part: ref.at[some(part)], lambda part: held.at[place, some(part)]

    enter, leave, finish = staged(
        heads,
        per_head,
        [(q_ref, q_held.at[0])],
        [(out_ref, out_held.at[0])],
        q_sems,
        out_sems,
        [feed(place, ref) for place, ref in enumerate(sources)],
        lambda place, part: sems.at[place, part],
    )
    tail = jnp.zeros((slots, 1, lanes), jnp.float32)
    for head in range(heads):
        enter(head)
        place = slice(head * per_head, (head + 1) * per_head)
        q = q_held[0, :, place, :].reshape(slots * per_head, dim)
        found = []
        for block in range(0, count, 2):
            scores = scores_of(q, held[block, head])
            high = jnp.max(scores, axis=1, keepdims=True)
            weights = jnp.exp(scores - high)
            den = jnp.sum(weights, axis=1, keepdims=True)
            found.append((high, den, times_values(weights, held[block + 1, head])))
        high = functools.reduce(jnp.maximum, [f[0] for f in found])
        factors = [jnp.exp(f[0] - high) for f in found]
        den = sum(factor * f[1] for factor, f in zip(factors, found))
        num = sum(f[2] * (factor / den) for factor, f in zip(factors, found))
        out_held[0, :, place, :] = num.reshape(slots, per_head, dim)
        tail = tail + head_lse(high + jnp.log(den), head, per_head, lanes)
        leave(head)
    out_held[0, :, lanes:, :] = tail_rows(split_lse(tail))
    finish()


def root_kernel(count, q_ref, q_far_ref, *refs):
    sources, out_refs = refs[:count], refs[count : count + 2]
    held, q_held, out_held, sems, q_sems, out_sems = refs[count + 2 :]
    requests, lanes, dim = q_ref.shape
    blocks, heads, half = held.shape[1], held.shape[2], held.shape[3] // 2
    per_head = lanes // heads
    group = heads // sems.shape[1]
    span = count * blocks * half

    def feed(place, ref):
        def some(part):
            return pl.ds(part * group, group)

        return lambda part: ref.at[:, some(part)], lambda part: held.at[place, :, some(part)]

    enter, leave, finish = staged(
        heads,
        per_head,
        [(ref, q_held.at[i]) for i, ref in enumerate((q_ref, q_far_ref))],
        [(ref, out_held.at[i]) for i, ref in enumerate(out_refs)],
        q_sems,
        out_sems,
        [feed(place, ref) for place, ref in enumerate(sources)],
        lambda place, part: sems.at[place, part],
    )
    tails = [jnp.zeros((requests, 1, lanes), jnp.float32) for _ in out_refs]
    for head in range(heads):
        enter(head)
        place = slice(head * per_head, (head + 1) * per_head)
        keys = held[:, :, head, :half, :].reshape(span, dim)
        values = held[:, :, head, half:, :].reshape(span, dim)
        for i in range(len(tails)):
            q = q_held[i, :, place, :].reshape(requests * per_head, dim)
            scores = scores_of(q, keys)
            high = jnp.max(scores, axis=1, keepdims=True)
            weights = jnp.exp(scores - high)
            den = jnp.sum(weights, axis=1, keepdims=True)
            num = times_values(weights, values) / den
            out_held[i, :, place, :] = num.reshape(requests, per_head, dim)
            tails[i] = tails[i] + head_lse(high + jnp.log(den), head, per_head, lanes)
        leave(head)
    for i, tail in enumerate(tails):
        out_held[i, :, lanes:, :] = tail_rows(split_lse(tail))
    finish()


def columns(table):
    lanes = table.shape[1]
    rest = jnp.zeros((lanes - table.shape[0], lanes), jnp.float32)
    return jnp.concatenate([table, rest], axis=0).T


def merge_kernel(idx_ref, part_ref, own_ref, far_ref, out_ref):
    sources, cap, _, lanes = part_ref.shape
    groups = own_ref.shape[0]
    lse_a = join_lse(own_ref[:, lanes:, :])
    lse_b = join_lse(far_ref[:, lanes:, :])
    high = jnp.maximum(lse_a, lse_b)
    factor_a = jnp.exp(lse_a - high)
    factor_b = jnp.exp(lse_b - high)
    total = factor_a + factor_b
    table = columns(jnp.concatenate([factor_a / total, factor_b / total], axis=0))
    pieces = split_lse(high + jnp.log(total))
    for r in range(groups):
        out_ref[r, :lanes, :] = (
            own_ref[r, :lanes, :] * table[:, r : r + 1]
            + far_ref[r, :lanes, :] * table[:, groups + r : groups + r + 1]
        )
        out_ref[r, lanes:, :] = tail_rows([piece[r : r + 1] for piece in pieces])
    for k in range(cap):
        reader = idx_ref[k]

        @pl.when(reader >= 0)
        def _():
            lse = join_lse(part_ref[:, k, lanes:, :])
            near = join_lse(out_ref[reader, lanes:, :])[None]
            high = jnp.maximum(jnp.max(lse, axis=0, keepdims=True), near)
            factor = jnp.exp(lse - high)
            near = jnp.exp(near - high)
            total = jnp.sum(factor, axis=0, keepdims=True) + near
            table = columns(jnp.concatenate([factor / total, near / total], axis=0))
            out = out_ref[reader, :lanes, :] * table[:, sources : sources + 1]
            for source in range(sources):
                out = out + part_ref[source, k, :lanes, :] * table[:, source : source + 1]
            out_ref[reader, :lanes, :] = out
            out_ref[reader, lanes:, :] = tail_rows(split_lse(high + jnp.log(total)))


def final_kernel(part_ref, local_ref, out_ref):
    groups, _, lanes = part_ref.shape
    lse = join_lse(part_ref[:, lanes:, :])
    near = local_ref[lanes : lanes + 1, :]
    high = jnp.maximum(jnp.max(lse, axis=0, keepdims=True), near)
    factor = jnp.exp(lse - high)
    near = jnp.exp(near - high)
    total = jnp.sum(factor, axis=0, keepdims=True) + near
    table = columns(jnp.concatenate([factor / total, near / total], axis=0))
    out = local_ref[:lanes, :] * table[:, groups : groups + 1]
    for source in range(groups):
        out = out + part_ref[source, :lanes, :] * table[:, source : source + 1]
    out_ref[...] = out.astype(out_ref.dtype)


def params(megabytes=48):
    return pltpu.CompilerParams(vmem_limit_bytes=megabytes * 1024 * 1024)


def estimate(area, dim, emphasis=1):
    return pl.CostEstimate(
        flops=emphasis * 4 * area * dim, bytes_accessed=6 * 1024 * 1024, transcendentals=area
    )


def vmem():
    return pl.BlockSpec(memory_space=pltpu.VMEM)


def anywhere():
    return pl.BlockSpec(memory_space=pl.ANY)


def smem():
    return pl.BlockSpec(memory_space=pltpu.SMEM)


def scratch(count, block, q, sets):
    return [
        pltpu.VMEM((count,) + block.shape, jnp.bfloat16),
        pltpu.VMEM((sets,) + q.shape, jnp.bfloat16),
        pltpu.VMEM((sets, q.shape[0], q.shape[1] + PAD, q.shape[2]), jnp.float32),
        pltpu.SemaphoreType.DMA((count, PARTS)),
        pltpu.SemaphoreType.DMA((sets,)),
        pltpu.SemaphoreType.DMA((sets, PARTS + 1)),
    ]


def exchange(blocks, axis):
    return lax.all_to_all(blocks, axis, split_axis=0, concat_axis=0, tiled=True)


def to_all(block, axis):
    return exchange(jnp.broadcast_to(block[None], (lax.axis_size(axis),) + block.shape), axis)


def shards(
    queries,
    root_keys,
    root_values,
    branch_keys,
    branch_values,
    suffix_keys,
    suffix_values,
    new_keys,
    new_values,
    branch_of,
    owner,
    suffix_len,
):
    steps, q_heads, dim = queries.shape[1:]
    heads = root_keys.shape[1]
    group = q_heads // heads
    per_head = steps * group
    rows = heads * per_head
    grp = lax.axis_size("grp")
    ring = lax.axis_size("z")
    core = lax.axis_size("core")
    spots = lax.axis_size("xhi") * ring * core
    grp_place = lax.axis_index("grp")
    seq_place = (lax.axis_index("xhi") * ring + lax.axis_index("z")) * core + lax.axis_index("core")
    swap = [(0, 1), (1, 0)]

    q_rows = queries[0].reshape(steps, heads, group, dim).transpose(1, 0, 2, 3)
    q_rows = q_rows.reshape(rows, dim)
    peers = to_all(q_rows, "grp")

    matches = branch_of[:, None] == jnp.arange(owner.shape[0])[None, :]
    slot_of = jnp.sum(jnp.where(matches, owner[None, :], 0), axis=1)
    slot_here = lax.dynamic_slice_in_dim(slot_of.reshape(grp, spots), seq_place, 1, 1)[:, 0]
    reading = slot_here == grp_place
    group_ids = jnp.arange(grp)
    before = jnp.sum((reading[None, :] & (group_ids[None, :] < group_ids[:, None])), axis=1)
    chosen = reading[None, :] & (before[None, :] == jnp.arange(CAP)[:, None])
    readers = jnp.max(jnp.where(chosen, group_ids[None, :], -1), axis=1).astype(jnp.int32)

    area = ring * CAP * rows * branch_keys.shape[1] * 4

    def gather_readers(peers):
        packed = pl.pallas_call(
            select_kernel,
            out_shape=jax.ShapeDtypeStruct((ring, CAP, rows, dim), jnp.bfloat16),
            grid_spec=pltpu.PrefetchScalarGridSpec(
                num_scalar_prefetch=1,
                grid=(CAP,),
                in_specs=[
                    pl.BlockSpec((1, rows, dim), lambda k, idx: (jnp.maximum(idx[k], 0), 0, 0))
                ],
                out_specs=pl.BlockSpec((ring, 1, rows, dim), lambda k, idx: (0, k, 0, 0)),
            ),
            compiler_params=params(),
            cost_estimate=estimate(area, dim, EMPHASIS),
            name="pick_readers",
        )(readers, peers)
        return exchange(packed, "z")

    keys_own = branch_keys[0].transpose(1, 0, 2)
    values_own = branch_values[0].transpose(1, 0, 2)
    root_block = jnp.concatenate([root_keys, root_values], axis=0).transpose(1, 0, 2)
    root_block = lax.optimization_barrier(root_block)
    root_own = lax.all_gather(root_block, "z")
    peers_far = lax.ppermute(peers, "xhi", swap)
    keys_far = lax.ppermute(keys_own, "xhi", swap)
    values_far = lax.ppermute(values_own, "xhi", swap)
    slots = gather_readers(peers)
    branch_blocks = [
        keys_own,
        values_own,
        lax.ppermute(keys_own, "core", swap),
        lax.ppermute(values_own, "core", swap),
        keys_far,
        values_far,
        lax.ppermute(keys_far, "core", swap),
        lax.ppermute(values_far, "core", swap),
    ]
    flat = suffix_keys.shape[1] * heads
    local = pl.pallas_call(
        functools.partial(local_kernel, heads),
        out_shape=jax.ShapeDtypeStruct((rows + PAD, dim), jnp.float32),
        in_specs=[smem()] + [vmem()] * 5,
        out_specs=vmem(),
        compiler_params=params(),
        cost_estimate=pl.CostEstimate(
            flops=4 * rows * flat * dim, bytes_accessed=4 * flat * dim, transcendentals=rows * flat
        ),
        name="local_attention",
    )(
        suffix_len,
        q_rows,
        suffix_keys.reshape(flat, dim),
        suffix_values.reshape(flat, dim),
        new_keys.reshape(steps * heads, dim),
        new_values.reshape(steps * heads, dim),
    )

    slots = slots.reshape(ring * CAP, rows, dim)
    area = ring * CAP * rows * branch_keys.shape[1] * 4
    count = len(branch_blocks)
    parts = pl.pallas_call(
        functools.partial(branch_kernel, count),
        out_shape=jax.ShapeDtypeStruct((ring * CAP, rows + PAD, dim), jnp.float32),
        in_specs=[anywhere()] * (1 + count),
        out_specs=anywhere(),
        scratch_shapes=scratch(count, keys_own, slots, 1),
        compiler_params=params(54),
        cost_estimate=estimate(area, dim),
        name="branch_attention",
    )(slots, *branch_blocks)
    parts = parts.astype(jnp.float16).reshape(ring, CAP, rows + PAD, dim)
    peers, peers_far, root_own, _ = lax.optimization_barrier((peers, peers_far, root_own, parts))
    root_blocks = [root_own, lax.ppermute(root_own, "core", swap)]
    parts = exchange(parts, "z")

    whole = jax.ShapeDtypeStruct((grp, rows + PAD, dim), jnp.float32)
    count = len(root_blocks)
    root, root_far = pl.pallas_call(
        functools.partial(root_kernel, count),
        out_shape=(whole, whole),
        in_specs=[anywhere()] * (2 + count),
        out_specs=(anywhere(), anywhere()),
        scratch_shapes=scratch(count, root_own, peers, 2),
        compiler_params=params(),
        cost_estimate=estimate(area, dim),
        name="root_attention",
    )(peers, peers_far, *root_blocks)
    root_far = lax.ppermute(root_far.astype(jnp.float16), "xhi", swap).astype(jnp.float32)
    parts, root, root_far = lax.optimization_barrier((parts, root, root_far))
    parts = parts.astype(jnp.float32)
    merged = pl.pallas_call(
        merge_kernel,
        out_shape=whole,
        in_specs=[smem()] + [vmem()] * 3,
        out_specs=vmem(),
        compiler_params=params(),
        name="merge_parts",
    )(readers, parts, root, root_far)
    back = exchange(merged.astype(jnp.float16), "grp").astype(jnp.float32)
    mine = pl.pallas_call(
        final_kernel,
        out_shape=jax.ShapeDtypeStruct((rows, dim), jnp.bfloat16),
        in_specs=[vmem()] * 2,
        out_specs=vmem(),
        compiler_params=params(),
        name="final_merge",
    )(back, local)
    mine = mine.reshape(heads, steps, group, dim).transpose(1, 0, 2, 3)
    return mine.reshape(queries.shape)


def solution(mesh):
    grp, seq = mesh.devices.shape
    fine = Mesh(mesh.devices.reshape(grp, 2, seq // 4, 2), ("grp", "xhi", "z", "core"))
    seq = ("xhi", "z", "core")
    both = ("grp",) + seq
    in_specs = (
        P(both, None, None, None),
        P(both, None, None),
        P(both, None, None),
        P("grp", seq, None, None),
        P("grp", seq, None, None),
        P(both, None, None, None),
        P(both, None, None, None),
        P(both, None, None, None),
        P(both, None, None, None),
        P(),
        P(),
        P(both),
    )
    out_specs = P(both, None, None, None)
    return jax.shard_map(shards, mesh=fine, in_specs=in_specs, out_specs=out_specs, check_vma=False)
```

```python
import functools
import math

import jax
import jax.numpy as jnp
from jax import lax
from jax.experimental import pallas as pl
from jax.experimental.pallas import tpu as pltpu
from jax.sharding import Mesh, PartitionSpec as P

CAP = 2
PAD = 8
LOW = -1e30
PARTS = 4
EMPHASIS = 18
NT = (((1,), (1,)), ((), ()))


def scores_of(rows, keys):
    raw = lax.dot_general(rows, keys, NT, preferred_element_type=jnp.float32)
    return raw * (1.0 / math.sqrt(keys.shape[-1]))


def times_values(weights, values):
    return jnp.dot(weights.astype(jnp.bfloat16), values, preferred_element_type=jnp.float32)


def head_lse(lse, head, per_head, lanes):
    lse = jnp.broadcast_to(lse, (lse.shape[0], lanes))
    row = lax.broadcasted_iota(jnp.int32, lse.shape, 0)
    col = lax.broadcasted_iota(jnp.int32, lse.shape, 1)
    lse = jnp.where(col == head * per_head + row % per_head, lse, 0.0)
    return jnp.sum(lse.reshape(-1, per_head, lanes), axis=1, keepdims=True)


def tail_rows(pieces):
    shape = pieces[0].shape[:-2] + (PAD, pieces[0].shape[-1])
    row = lax.broadcasted_iota(jnp.int32, shape, len(shape) - 2)
    out = jnp.zeros(shape, jnp.float32)
    for place, piece in enumerate(pieces):
        out = jnp.where(row == place, jnp.broadcast_to(piece, shape), out)
    return out


def split_lse(lse):
    coarse = jnp.round(lse * 0.25) * 4.0
    rest = lse - coarse
    middle = jnp.round(rest * 512.0) * (1.0 / 512.0)
    return coarse, middle, rest - middle


def join_lse(tail):
    return tail[..., 0, :] + tail[..., 1, :] + tail[..., 2, :]


def local_kernel(heads, len_ref, q_ref, k_ref, v_ref, nk_ref, nv_ref, out_ref):
    rows = q_ref.shape[0]
    per_head = rows // heads
    q = q_ref[...]
    far = scores_of(q, k_ref[...])
    row = lax.broadcasted_iota(jnp.int32, far.shape, 0)
    col = lax.broadcasted_iota(jnp.int32, far.shape, 1)
    seen = (col % heads == row // per_head) & (col < len_ref[0] * heads)
    far = jnp.where(seen, far, LOW)
    near = scores_of(q, nk_ref[...])
    row = lax.broadcasted_iota(jnp.int32, near.shape, 0)
    col = lax.broadcasted_iota(jnp.int32, near.shape, 1)
    steps = near.shape[1] // heads
    step = (row % per_head) // (per_head // steps)
    seen = (col % heads == row // per_head) & (col // heads <= step)
    near = jnp.where(seen, near, LOW)
    high = jnp.maximum(
        jnp.max(far, axis=1, keepdims=True), jnp.max(near, axis=1, keepdims=True)
    )
    far = jnp.exp(far - high)
    near = jnp.exp(near - high)
    den = jnp.sum(far, axis=1, keepdims=True) + jnp.sum(near, axis=1, keepdims=True)
    num = times_values(far, v_ref[...]) + times_values(near, nv_ref[...])
    out_ref[:rows, :] = num / den
    lse = jnp.broadcast_to(high + jnp.log(den), (rows, rows))
    row = lax.broadcasted_iota(jnp.int32, (rows, rows), 0)
    col = lax.broadcasted_iota(jnp.int32, (rows, rows), 1)
    flat = jnp.sum(jnp.where(row == col, lse, 0.0), axis=0, keepdims=True)
    out_ref[rows:, :] = jnp.broadcast_to(flat, (PAD, rows))


def select_kernel(idx_ref, peer_ref, out_ref):
    out_ref[...] = jnp.broadcast_to(peer_ref[...][None], out_ref.shape)


def staged(heads, per_head, q_ref, out_ref, q_held, out_held, q_sem, out_sems, feeds, feed_sem):
    parts = out_sems.shape[0] - 1
    group = heads // parts
    reads = [
        [
            pltpu.make_async_copy(source(part), target(part), feed_sem(place, part))
            for place, (source, target) in enumerate(feeds)
        ]
        for part in range(parts)
    ]
    q_copy = pltpu.make_async_copy(q_ref, q_held, q_sem)
    q_copy.start()
    for copies in reads:
        for copy in copies:
            copy.start()
    q_copy.wait()
    span = group * per_head
    writes = [
        pltpu.make_async_copy(
            out_held.at[:, pl.ds(part * span, span), :],
            out_ref.at[:, pl.ds(part * span, span), :],
            out_sems.at[part],
        )
        for part in range(parts)
    ]
    tail = pl.ds(heads * per_head, PAD)
    writes.append(
        pltpu.make_async_copy(
            out_held.at[:, tail, :], out_ref.at[:, tail, :], out_sems.at[parts]
        )
    )

    def enter(head):
        if head % group == 0:
            for copy in reads[head // group]:
                copy.wait()

    def leave(head):
        if (head + 1) % group == 0:
            writes[head // group].start()

    def finish():
        writes[-1].start()
        for copy in writes:
            copy.wait()

    return enter, leave, finish


def branch_kernel(count, q_ref, *refs):
    sources, out_ref = refs[:count], refs[count]
    held, q_held, out_held, sems, q_sem, out_sems = refs[count + 1 :]
    slots, lanes, dim = q_ref.shape
    heads = sources[0].shape[0]
    per_head = lanes // heads
    group = heads // sems.shape[1]

    def feed(place, ref):
        def some(part):
            return pl.ds(part * group, group)

        return lambda part: ref.at[some(part)], lambda part: held.at[place, some(part)]

    enter, leave, finish = staged(
        heads,
        per_head,
        q_ref,
        out_ref,
        q_held,
        out_held,
        q_sem,
        out_sems,
        [feed(place, ref) for place, ref in enumerate(sources)],
        lambda place, part: sems.at[place, part],
    )
    tail = jnp.zeros((slots, 1, lanes), jnp.float32)
    for head in range(heads):
        enter(head)
        place = slice(head * per_head, (head + 1) * per_head)
        q = q_held[:, place, :].reshape(slots * per_head, dim)
        found = []
        for block in range(0, count, 2):
            scores = scores_of(q, held[block, head])
            high = jnp.max(scores, axis=1, keepdims=True)
            weights = jnp.exp(scores - high)
            den = jnp.sum(weights, axis=1, keepdims=True)
            found.append((high, den, times_values(weights, held[block + 1, head])))
        high = functools.reduce(jnp.maximum, [f[0] for f in found])
        factors = [jnp.exp(f[0] - high) for f in found]
        den = sum(factor * f[1] for factor, f in zip(factors, found))
        num = sum(f[2] * (factor / den) for factor, f in zip(factors, found))
        out_held[:, place, :] = num.reshape(slots, per_head, dim)
        tail = tail + head_lse(high + jnp.log(den), head, per_head, lanes)
        leave(head)
    out_held[:, lanes:, :] = tail_rows(split_lse(tail))
    finish()


def root_kernel(count, q_ref, *refs):
    sources, out_ref = refs[:count], refs[count]
    held, q_held, out_held, sems, q_sem, out_sems = refs[count + 1 :]
    requests, lanes, dim = q_ref.shape
    blocks, heads, half = held.shape[1], held.shape[2], held.shape[3] // 2
    per_head = lanes // heads
    group = heads // sems.shape[1]
    span = blocks * half

    def feed(place, ref):
        def some(part):
            return pl.ds(part * group, group)

        return lambda part: ref.at[:, some(part)], lambda part: held.at[place, :, some(part)]

    enter, leave, finish = staged(
        heads,
        per_head,
        q_ref,
        out_ref,
        q_held,
        out_held,
        q_sem,
        out_sems,
        [feed(place, ref) for place, ref in enumerate(sources)],
        lambda place, part: sems.at[place, part],
    )
    tail = jnp.zeros((requests, 1, lanes), jnp.float32)
    for head in range(heads):
        enter(head)
        place = slice(head * per_head, (head + 1) * per_head)
        q = q_held[:, place, :].reshape(requests * per_head, dim)
        scores = [scores_of(q, held[i, :, head, :half, :].reshape(span, dim)) for i in range(count)]
        high = functools.reduce(
            jnp.maximum, [jnp.max(s, axis=1, keepdims=True) for s in scores]
        )
        weights = [jnp.exp(s - high) for s in scores]
        den = sum(jnp.sum(w, axis=1, keepdims=True) for w in weights)
        num = sum(
            times_values(w, held[i, :, head, half:, :].reshape(span, dim))
            for i, w in enumerate(weights)
        )
        out_held[:, place, :] = (num / den).reshape(requests, per_head, dim)
        tail = tail + head_lse(high + jnp.log(den), head, per_head, lanes)
        leave(head)
    out_held[:, lanes:, :] = tail_rows(split_lse(tail))
    finish()


def columns(table):
    lanes = table.shape[1]
    rest = jnp.zeros((lanes - table.shape[0], lanes), jnp.float32)
    return jnp.concatenate([table, rest], axis=0).T


def merge_kernel(idx_ref, part_ref, root_ref, out_ref):
    sources, cap, _, lanes = part_ref.shape
    out_ref[...] = root_ref[...]
    for k in range(cap):
        reader = idx_ref[k]

        @pl.when(reader >= 0)
        def _():
            lse = join_lse(part_ref[:, k, lanes:, :])
            near = join_lse(out_ref[reader, lanes:, :])[None]
            high = jnp.maximum(jnp.max(lse, axis=0, keepdims=True), near)
            factor = jnp.exp(lse - high)
            near = jnp.exp(near - high)
            total = jnp.sum(factor, axis=0, keepdims=True) + near
            table = columns(jnp.concatenate([factor / total, near / total], axis=0))
            out = out_ref[reader, :lanes, :] * table[:, sources : sources + 1]
            for source in range(sources):
                out = out + part_ref[source, k, :lanes, :] * table[:, source : source + 1]
            out_ref[reader, :lanes, :] = out
            out_ref[reader, lanes:, :] = tail_rows(split_lse(high + jnp.log(total)))


def final_kernel(part_ref, local_ref, out_ref):
    groups, _, lanes = part_ref.shape
    lse = join_lse(part_ref[:, lanes:, :])
    near = local_ref[lanes : lanes + 1, :]
    high = jnp.maximum(jnp.max(lse, axis=0, keepdims=True), near)
    factor = jnp.exp(lse - high)
    near = jnp.exp(near - high)
    total = jnp.sum(factor, axis=0, keepdims=True) + near
    table = columns(jnp.concatenate([factor / total, near / total], axis=0))
    out = local_ref[:lanes, :] * table[:, groups : groups + 1]
    for source in range(groups):
        out = out + part_ref[source, :lanes, :] * table[:, source : source + 1]
    out_ref[...] = out.astype(out_ref.dtype)


def params(megabytes=48):
    return pltpu.CompilerParams(vmem_limit_bytes=megabytes * 1024 * 1024)


def estimate(area, dim, emphasis=1):
    return pl.CostEstimate(
        flops=emphasis * 4 * area * dim, bytes_accessed=6 * 1024 * 1024, transcendentals=area
    )


def vmem():
    return pl.BlockSpec(memory_space=pltpu.VMEM)


def anywhere():
    return pl.BlockSpec(memory_space=pl.ANY)


def smem():
    return pl.BlockSpec(memory_space=pltpu.SMEM)


def scratch(count, block, q):
    return [
        pltpu.VMEM((count,) + block.shape, jnp.bfloat16),
        pltpu.VMEM(q.shape, jnp.bfloat16),
        pltpu.VMEM((q.shape[0], q.shape[1] + PAD, q.shape[2]), jnp.float32),
        pltpu.SemaphoreType.DMA((count, PARTS)),
        pltpu.SemaphoreType.DMA(()),
        pltpu.SemaphoreType.DMA((PARTS + 1,)),
    ]


def exchange(blocks, axis):
    return lax.all_to_all(blocks, axis, split_axis=0, concat_axis=0, tiled=True)


def to_all(block, axis):
    return exchange(jnp.broadcast_to(block[None], (lax.axis_size(axis),) + block.shape), axis)


def shards(
    queries,
    root_keys,
    root_values,
    branch_keys,
    branch_values,
    suffix_keys,
    suffix_values,
    new_keys,
    new_values,
    branch_of,
    owner,
    suffix_len,
):
    steps, q_heads, dim = queries.shape[1:]
    heads = root_keys.shape[1]
    group = q_heads // heads
    per_head = steps * group
    rows = heads * per_head
    grp = lax.axis_size("grp")
    ring = lax.axis_size("z")
    core = lax.axis_size("core")
    spots = lax.axis_size("xhi") * ring * core
    grp_place = lax.axis_index("grp")
    seq_place = (lax.axis_index("xhi") * ring + lax.axis_index("z")) * core + lax.axis_index("core")
    swap = [(0, 1), (1, 0)]

    q_rows = queries[0].reshape(steps, heads, group, dim).transpose(1, 0, 2, 3)
    q_rows = q_rows.reshape(rows, dim)
    peers = to_all(q_rows, "grp")

    matches = branch_of[:, None] == jnp.arange(owner.shape[0])[None, :]
    slot_of = jnp.sum(jnp.where(matches, owner[None, :], 0), axis=1)
    slot_here = lax.dynamic_slice_in_dim(slot_of.reshape(grp, spots), seq_place, 1, 1)[:, 0]
    reading = slot_here == grp_place
    group_ids = jnp.arange(grp)
    before = jnp.sum((reading[None, :] & (group_ids[None, :] < group_ids[:, None])), axis=1)
    chosen = reading[None, :] & (before[None, :] == jnp.arange(CAP)[:, None])
    readers = jnp.max(jnp.where(chosen, group_ids[None, :], -1), axis=1).astype(jnp.int32)

    area = ring * CAP * rows * branch_keys.shape[1] * 4

    def gather_readers(peers):
        packed = pl.pallas_call(
            select_kernel,
            out_shape=jax.ShapeDtypeStruct((ring, CAP, rows, dim), jnp.bfloat16),
            grid_spec=pltpu.PrefetchScalarGridSpec(
                num_scalar_prefetch=1,
                grid=(CAP,),
                in_specs=[
                    pl.BlockSpec((1, rows, dim), lambda k, idx: (jnp.maximum(idx[k], 0), 0, 0))
                ],
                out_specs=pl.BlockSpec((ring, 1, rows, dim), lambda k, idx: (0, k, 0, 0)),
            ),
            compiler_params=params(),
            cost_estimate=estimate(area, dim, EMPHASIS),
            name="pick_readers",
        )(readers, peers)
        return exchange(packed, "z")

    root_block = jnp.concatenate([root_keys, root_values], axis=0).transpose(1, 0, 2)
    pair = jnp.stack([root_block, lax.ppermute(root_block, "xhi", swap)])
    pair, keys_own, values_own = lax.optimization_barrier((pair, branch_keys[0], branch_values[0]))
    root_own = lax.all_gather(pair, "z", axis=0, tiled=True)
    keys_own = keys_own.transpose(1, 0, 2)
    values_own = values_own.transpose(1, 0, 2)
    peers, _ = lax.optimization_barrier((peers, pair))
    keys_far = lax.ppermute(keys_own, "xhi", swap)
    values_far = lax.ppermute(values_own, "xhi", swap)
    slots = gather_readers(peers)
    branch_blocks = [
        keys_own,
        values_own,
        lax.ppermute(keys_own, "core", swap),
        lax.ppermute(values_own, "core", swap),
        keys_far,
        values_far,
        lax.ppermute(keys_far, "core", swap),
        lax.ppermute(values_far, "core", swap),
    ]
    flat = suffix_keys.shape[1] * heads
    local = pl.pallas_call(
        functools.partial(local_kernel, heads),
        out_shape=jax.ShapeDtypeStruct((rows + PAD, dim), jnp.float32),
        in_specs=[smem()] + [vmem()] * 5,
        out_specs=vmem(),
        compiler_params=params(),
        cost_estimate=pl.CostEstimate(
            flops=4 * rows * flat * dim, bytes_accessed=4 * flat * dim, transcendentals=rows * flat
        ),
        name="local_attention",
    )(
        suffix_len,
        q_rows,
        suffix_keys.reshape(flat, dim),
        suffix_values.reshape(flat, dim),
        new_keys.reshape(steps * heads, dim),
        new_values.reshape(steps * heads, dim),
    )

    slots = slots.reshape(ring * CAP, rows, dim)
    area = ring * CAP * rows * branch_keys.shape[1] * 4
    count = len(branch_blocks)
    parts = pl.pallas_call(
        functools.partial(branch_kernel, count),
        out_shape=jax.ShapeDtypeStruct((ring * CAP, rows + PAD, dim), jnp.float32),
        in_specs=[anywhere()] * (1 + count),
        out_specs=anywhere(),
        scratch_shapes=scratch(count, keys_own, slots),
        compiler_params=params(54),
        cost_estimate=estimate(area, dim),
        name="branch_attention",
    )(slots, *branch_blocks)
    parts = parts.astype(jnp.float16).reshape(ring, CAP, rows + PAD, dim)
    peers, root_own, _ = lax.optimization_barrier((peers, root_own, parts))
    root_blocks = [root_own, lax.ppermute(root_own, "core", swap)]
    parts = exchange(parts, "z")

    whole = jax.ShapeDtypeStruct((grp, rows + PAD, dim), jnp.float32)
    count = len(root_blocks)
    root = pl.pallas_call(
        functools.partial(root_kernel, count),
        out_shape=whole,
        in_specs=[anywhere()] * (1 + count),
        out_specs=anywhere(),
        scratch_shapes=scratch(count, root_own, peers),
        compiler_params=params(),
        cost_estimate=estimate(area, dim),
        name="root_attention",
    )(peers, *root_blocks)
    parts, root = lax.optimization_barrier((parts, root))
    parts = parts.astype(jnp.float32)
    merged = pl.pallas_call(
        merge_kernel,
        out_shape=whole,
        in_specs=[smem()] + [vmem()] * 2,
        out_specs=vmem(),
        compiler_params=params(),
        name="merge_parts",
    )(readers, parts, root)
    back = exchange(merged.astype(jnp.float16), "grp").astype(jnp.float32)
    mine = pl.pallas_call(
        final_kernel,
        out_shape=jax.ShapeDtypeStruct((rows, dim), jnp.bfloat16),
        in_specs=[vmem()] * 2,
        out_specs=vmem(),
        compiler_params=params(),
        name="final_merge",
    )(back, local)
    mine = mine.reshape(heads, steps, group, dim).transpose(1, 0, 2, 3)
    return mine.reshape(queries.shape)


def solution(mesh):
    grp, seq = mesh.devices.shape
    fine = Mesh(mesh.devices.reshape(grp, 2, seq // 4, 2), ("grp", "xhi", "z", "core"))
    seq = ("xhi", "z", "core")
    both = ("grp",) + seq
    in_specs = (
        P(both, None, None, None),
        P(both, None, None),
        P(both, None, None),
        P("grp", seq, None, None),
        P("grp", seq, None, None),
        P(both, None, None, None),
        P(both, None, None, None),
        P(both, None, None, None),
        P(both, None, None, None),
        P(),
        P(),
        P(both),
    )
    out_specs = P(both, None, None, None)
    return jax.shard_map(shards, mesh=fine, in_specs=in_specs, out_specs=out_specs, check_vma=False)
```

```python
import functools
import math

import jax
import jax.numpy as jnp
from jax import lax
from jax.experimental import pallas as pl
from jax.experimental.pallas import tpu as pltpu
from jax.sharding import Mesh, PartitionSpec as P

CAP = 2
PAD = 8
LOW = -1e30
PARTS = 4
SPLITS = 4
EMPHASIS = 24
NT = (((1,), (1,)), ((), ()))


def scores_of(rows, keys):
    raw = lax.dot_general(rows, keys, NT, preferred_element_type=jnp.float32)
    return raw * (1.0 / math.sqrt(keys.shape[-1]))


def times_values(weights, values):
    return jnp.dot(weights.astype(jnp.bfloat16), values, preferred_element_type=jnp.float32)


def head_lse(lse, head, per_head, lanes):
    lse = jnp.broadcast_to(lse, (lse.shape[0], lanes))
    row = lax.broadcasted_iota(jnp.int32, lse.shape, 0)
    col = lax.broadcasted_iota(jnp.int32, lse.shape, 1)
    lse = jnp.where(col == head * per_head + row % per_head, lse, 0.0)
    return jnp.sum(lse.reshape(-1, per_head, lanes), axis=1, keepdims=True)


def tail_rows(pieces):
    shape = pieces[0].shape[:-2] + (PAD, pieces[0].shape[-1])
    row = lax.broadcasted_iota(jnp.int32, shape, len(shape) - 2)
    out = jnp.zeros(shape, jnp.float32)
    for place, piece in enumerate(pieces):
        out = jnp.where(row == place, jnp.broadcast_to(piece, shape), out)
    return out


def split_lse(lse):
    coarse = jnp.round(lse * 0.25) * 4.0
    rest = lse - coarse
    middle = jnp.round(rest * 512.0) * (1.0 / 512.0)
    return coarse, middle, rest - middle


def join_lse(tail):
    return tail[..., 0, :] + tail[..., 1, :] + tail[..., 2, :]


def local_kernel(heads, len_ref, q_ref, k_ref, v_ref, nk_ref, nv_ref, out_ref):
    rows = q_ref.shape[0]
    per_head = rows // heads
    q = q_ref[...]
    far = scores_of(q, k_ref[...])
    row = lax.broadcasted_iota(jnp.int32, far.shape, 0)
    col = lax.broadcasted_iota(jnp.int32, far.shape, 1)
    seen = (col % heads == row // per_head) & (col < len_ref[0] * heads)
    far = jnp.where(seen, far, LOW)
    near = scores_of(q, nk_ref[...])
    row = lax.broadcasted_iota(jnp.int32, near.shape, 0)
    col = lax.broadcasted_iota(jnp.int32, near.shape, 1)
    steps = near.shape[1] // heads
    step = (row % per_head) // (per_head // steps)
    seen = (col % heads == row // per_head) & (col // heads <= step)
    near = jnp.where(seen, near, LOW)
    high = jnp.maximum(
        jnp.max(far, axis=1, keepdims=True), jnp.max(near, axis=1, keepdims=True)
    )
    far = jnp.exp(far - high)
    near = jnp.exp(near - high)
    den = jnp.sum(far, axis=1, keepdims=True) + jnp.sum(near, axis=1, keepdims=True)
    num = times_values(far, v_ref[...]) + times_values(near, nv_ref[...])
    out_ref[:rows, :] = num / den
    lse = jnp.broadcast_to(high + jnp.log(den), (rows, rows))
    row = lax.broadcasted_iota(jnp.int32, (rows, rows), 0)
    col = lax.broadcasted_iota(jnp.int32, (rows, rows), 1)
    flat = jnp.sum(jnp.where(row == col, lse, 0.0), axis=0, keepdims=True)
    out_ref[rows:, :] = jnp.broadcast_to(flat, (PAD, rows))


def select_kernel(idx_ref, peer_ref, out_ref):
    out_ref[...] = jnp.broadcast_to(peer_ref[...][None], out_ref.shape)


def branch_kernel(count, q_ref, *refs):
    sources, out_ref, held, sems = refs[:count], refs[count], refs[count + 1], refs[count + 2]
    slots, lanes, dim = q_ref.shape
    heads = sources[0].shape[0]
    per_head = lanes // heads
    group = heads // PARTS

    def copies(part):
        some = pl.ds(part * group, group)
        return [
            pltpu.make_async_copy(ref.at[some], held.at[place, some], sems.at[place, part])
            for place, ref in enumerate(sources)
        ]

    for part in range(PARTS):
        for place, copy in enumerate(copies(part)):
            copy.start(priority=place % 2)
    tail = jnp.zeros((slots, 1, lanes), jnp.float32)
    for head in range(heads):
        if head % group == 0:
            for copy in copies(head // group):
                copy.wait()
        place = slice(head * per_head, (head + 1) * per_head)
        q = q_ref[:, place, :].reshape(slots * per_head, dim)
        found = []
        for block in range(0, count, 2):
            scores = scores_of(q, held[block, head])
            high = jnp.max(scores, axis=1, keepdims=True)
            weights = jnp.exp(scores - high)
            den = jnp.sum(weights, axis=1, keepdims=True)
            found.append((high, den, times_values(weights, held[block + 1, head])))
        high = functools.reduce(jnp.maximum, [f[0] for f in found])
        factors = [jnp.exp(f[0] - high) for f in found]
        den = sum(factor * f[1] for factor, f in zip(factors, found))
        num = sum(f[2] * (factor / den) for factor, f in zip(factors, found))
        out_ref[:, place, :] = num.reshape(slots, per_head, dim)
        tail = tail + head_lse(high + jnp.log(den), head, per_head, lanes)
    out_ref[:, lanes:, :] = tail_rows(split_lse(tail))


def root_kernel(count, q_ref, *refs):
    sources, out_ref, held, sems = refs[:count], refs[count], refs[count + 1], refs[count + 2]
    requests, lanes, dim = q_ref.shape
    blocks, heads, half = held.shape[0], held.shape[1], held.shape[2] // 2
    per_head = lanes // heads
    group = heads // PARTS
    span = blocks * half
    offsets = [sum(ref.shape[0] for ref in sources[:place]) for place in range(count)]

    def copies(part):
        some = pl.ds(part * group, group)
        return [
            pltpu.make_async_copy(
                ref.at[:, some], held.at[pl.ds(offset, ref.shape[0]), some], sems.at[place, part]
            )
            for place, (ref, offset) in enumerate(zip(sources, offsets))
        ]

    for part in range(PARTS):
        for place, copy in enumerate(copies(part)):
            copy.start(priority=place % 2)
    tail = jnp.zeros((requests, 1, lanes), jnp.float32)
    for head in range(heads):
        if head % group == 0:
            for copy in copies(head // group):
                copy.wait()
        place = slice(head * per_head, (head + 1) * per_head)
        q = q_ref[:, place, :].reshape(requests * per_head, dim)
        scores = scores_of(q, held[:, head, :half, :].reshape(span, dim))
        high = jnp.max(scores, axis=1, keepdims=True)
        weights = jnp.exp(scores - high)
        den = jnp.sum(weights, axis=1, keepdims=True)
        num = times_values(weights, held[:, head, half:, :].reshape(span, dim)) / den
        out_ref[:, place, :] = num.reshape(requests, per_head, dim)
        tail = tail + head_lse(high + jnp.log(den), head, per_head, lanes)
    out_ref[:, lanes:, :] = tail_rows(split_lse(tail))


def columns(table):
    lanes = table.shape[1]
    rest = jnp.zeros((lanes - table.shape[0], lanes), jnp.float32)
    return jnp.concatenate([table, rest], axis=0).T


def merge_kernel(idx_ref, part_ref, root_ref, out_ref):
    sources, cap, _, lanes = part_ref.shape
    out_ref[...] = root_ref[...]
    for k in range(cap):
        reader = idx_ref[k]

        @pl.when(reader >= 0)
        def _():
            lse = join_lse(part_ref[:, k, lanes:, :])
            near = join_lse(out_ref[reader, lanes:, :])[None]
            high = jnp.maximum(jnp.max(lse, axis=0, keepdims=True), near)
            factor = jnp.exp(lse - high)
            near = jnp.exp(near - high)
            total = jnp.sum(factor, axis=0, keepdims=True) + near
            table = columns(jnp.concatenate([factor / total, near / total], axis=0))
            out = out_ref[reader, :lanes, :] * table[:, sources : sources + 1]
            for source in range(sources):
                out = out + part_ref[source, k, :lanes, :] * table[:, source : source + 1]
            out_ref[reader, :lanes, :] = out
            out_ref[reader, lanes:, :] = tail_rows(split_lse(high + jnp.log(total)))


def final_kernel(part_ref, local_ref, out_ref):
    groups, _, lanes = part_ref.shape
    lse = join_lse(part_ref[:, lanes:, :])
    near = local_ref[lanes : lanes + 1, :]
    high = jnp.maximum(jnp.max(lse, axis=0, keepdims=True), near)
    factor = jnp.exp(lse - high)
    near = jnp.exp(near - high)
    total = jnp.sum(factor, axis=0, keepdims=True) + near
    table = columns(jnp.concatenate([factor / total, near / total], axis=0))
    out = local_ref[:lanes, :] * table[:, groups : groups + 1]
    for source in range(groups):
        out = out + part_ref[source, :lanes, :] * table[:, source : source + 1]
    out_ref[...] = out.astype(out_ref.dtype)


def params(megabytes=20):
    return pltpu.CompilerParams(vmem_limit_bytes=megabytes * 1024 * 1024)


def estimate(area, dim, emphasis=1):
    return pl.CostEstimate(
        flops=emphasis * 4 * area * dim, bytes_accessed=6 * 1024 * 1024, transcendentals=area
    )


def vmem():
    return pl.BlockSpec(memory_space=pltpu.VMEM)


def hbm():
    return pl.BlockSpec(memory_space=pltpu.HBM)


def smem():
    return pl.BlockSpec(memory_space=pltpu.SMEM)


def scratch(count, shape):
    return [pltpu.VMEM(shape, jnp.bfloat16), pltpu.SemaphoreType.DMA((count, PARTS))]


def in_hbm(blocks):
    return [pltpu.with_memory_space_constraint(block, pltpu.HBM) for block in blocks]


def exchange(blocks, axis):
    return lax.all_to_all(blocks, axis, split_axis=0, concat_axis=0, tiled=True)


def to_all(block, axis):
    return exchange(jnp.broadcast_to(block[None], (lax.axis_size(axis),) + block.shape), axis)


def shards(
    queries,
    root_keys,
    root_values,
    branch_keys,
    branch_values,
    suffix_keys,
    suffix_values,
    new_keys,
    new_values,
    branch_of,
    owner,
    suffix_len,
):
    steps, q_heads, dim = queries.shape[1:]
    heads = root_keys.shape[1]
    group = q_heads // heads
    per_head = steps * group
    rows = heads * per_head
    grp = lax.axis_size("grp")
    ring = lax.axis_size("z")
    core = lax.axis_size("core")
    spots = lax.axis_size("xhi") * ring * core
    grp_place = lax.axis_index("grp")
    seq_place = (lax.axis_index("xhi") * ring + lax.axis_index("z")) * core + lax.axis_index("core")
    swap = [(0, 1), (1, 0)]

    q_rows = queries[0].reshape(steps, heads, group, dim).transpose(1, 0, 2, 3)
    q_rows = q_rows.reshape(rows, dim)
    peers = to_all(q_rows, "grp")

    matches = branch_of[:, None] == jnp.arange(owner.shape[0])[None, :]
    slot_of = jnp.sum(jnp.where(matches, owner[None, :], 0), axis=1)
    slot_here = lax.dynamic_slice_in_dim(slot_of.reshape(grp, spots), seq_place, 1, 1)[:, 0]
    reading = slot_here == grp_place
    group_ids = jnp.arange(grp)
    before = jnp.sum((reading[None, :] & (group_ids[None, :] < group_ids[:, None])), axis=1)
    chosen = reading[None, :] & (before[None, :] == jnp.arange(CAP)[:, None])
    readers = jnp.max(jnp.where(chosen, group_ids[None, :], -1), axis=1).astype(jnp.int32)

    area = ring * CAP * rows * branch_keys.shape[1] * 4

    def gather_readers(peers):
        packed = pl.pallas_call(
            select_kernel,
            out_shape=jax.ShapeDtypeStruct((ring, CAP, rows, dim), jnp.bfloat16),
            grid_spec=pltpu.PrefetchScalarGridSpec(
                num_scalar_prefetch=1,
                grid=(CAP,),
                in_specs=[
                    pl.BlockSpec((1, rows, dim), lambda k, idx: (jnp.maximum(idx[k], 0), 0, 0))
                ],
                out_specs=pl.BlockSpec((ring, 1, rows, dim), lambda k, idx: (0, k, 0, 0)),
            ),
            compiler_params=params(),
            cost_estimate=estimate(area, dim, EMPHASIS),
            name="pick_readers",
        )(readers, peers)
        return exchange(packed, "z")

    root_block = jnp.concatenate([root_keys, root_values], axis=0).transpose(1, 0, 2)
    pair = jnp.stack([root_block, lax.ppermute(root_block, "xhi", swap)])
    pair, keys_own, values_own = lax.optimization_barrier((pair, branch_keys[0], branch_values[0]))
    root_own = lax.all_gather(pair, "z", axis=0, tiled=True)
    keys_own = keys_own.transpose(1, 0, 2)
    values_own = values_own.transpose(1, 0, 2)
    peers, _ = lax.optimization_barrier((peers, pair))
    keys_far = lax.ppermute(keys_own, "xhi", swap)
    values_far = lax.ppermute(values_own, "xhi", swap)
    slots = gather_readers(peers)
    branch_blocks = [
        keys_own,
        values_own,
        lax.ppermute(keys_own, "core", swap),
        lax.ppermute(values_own, "core", swap),
        keys_far,
        values_far,
        lax.ppermute(keys_far, "core", swap),
        lax.ppermute(values_far, "core", swap),
    ]
    flat = suffix_keys.shape[1] * heads
    local = pl.pallas_call(
        functools.partial(local_kernel, heads),
        out_shape=jax.ShapeDtypeStruct((rows + PAD, dim), jnp.float32),
        in_specs=[smem()] + [vmem()] * 5,
        out_specs=vmem(),
        compiler_params=params(),
        cost_estimate=pl.CostEstimate(
            flops=4 * rows * flat * dim, bytes_accessed=4 * flat * dim, transcendentals=rows * flat
        ),
        name="local_attention",
    )(
        suffix_len,
        q_rows,
        suffix_keys.reshape(flat, dim),
        suffix_values.reshape(flat, dim),
        new_keys.reshape(steps * heads, dim),
        new_values.reshape(steps * heads, dim),
    )

    slots = slots.reshape(ring * CAP, rows, dim)
    area = ring * CAP * rows * branch_keys.shape[1] * 4
    count = len(branch_blocks)
    parts = pl.pallas_call(
        functools.partial(branch_kernel, count),
        out_shape=jax.ShapeDtypeStruct((ring * CAP, rows + PAD, dim), jnp.float32),
        in_specs=[vmem()] + [hbm()] * count,
        out_specs=vmem(),
        scratch_shapes=scratch(count, (count,) + keys_own.shape),
        compiler_params=params(),
        cost_estimate=estimate(area, dim),
        name="branch_attention",
    )(slots, *in_hbm(branch_blocks))
    parts = parts.astype(jnp.float16).reshape(ring, CAP, rows + PAD, dim)
    peers, root_own, _ = lax.optimization_barrier((peers, root_own, parts))
    root_blocks = [root_own]
    root_blocks += [lax.ppermute(some, "core", swap) for some in jnp.split(root_own, SPLITS)]
    parts = exchange(parts, "z")

    whole = jax.ShapeDtypeStruct((grp, rows + PAD, dim), jnp.float32)
    count = len(root_blocks)
    root = pl.pallas_call(
        functools.partial(root_kernel, count),
        out_shape=whole,
        in_specs=[vmem()] + [hbm()] * count,
        out_specs=vmem(),
        scratch_shapes=scratch(count, (core * root_own.shape[0],) + root_own.shape[1:]),
        compiler_params=params(),
        cost_estimate=estimate(area, dim),
        name="root_attention",
    )(peers, *in_hbm(root_blocks))
    parts, root = lax.optimization_barrier((parts, root))
    parts = parts.astype(jnp.float32)
    merged = pl.pallas_call(
        merge_kernel,
        out_shape=whole,
        in_specs=[smem()] + [vmem()] * 2,
        out_specs=vmem(),
        compiler_params=params(),
        name="merge_parts",
    )(readers, parts, root)
    back = exchange(merged.astype(jnp.float16), "grp").astype(jnp.float32)
    mine = pl.pallas_call(
        final_kernel,
        out_shape=jax.ShapeDtypeStruct((rows, dim), jnp.bfloat16),
        in_specs=[vmem()] * 2,
        out_specs=vmem(),
        compiler_params=params(),
        name="final_merge",
    )(back, local)
    mine = mine.reshape(heads, steps, group, dim).transpose(1, 0, 2, 3)
    return mine.reshape(queries.shape)


def solution(mesh):
    grp, seq = mesh.devices.shape
    fine = Mesh(mesh.devices.reshape(grp, 2, seq // 4, 2), ("grp", "xhi", "z", "core"))
    seq = ("xhi", "z", "core")
    both = ("grp",) + seq
    in_specs = (
        P(both, None, None, None),
        P(both, None, None),
        P(both, None, None),
        P("grp", seq, None, None),
        P("grp", seq, None, None),
        P(both, None, None, None),
        P(both, None, None, None),
        P(both, None, None, None),
        P(both, None, None, None),
        P(),
        P(),
        P(both),
    )
    out_specs = P(both, None, None, None)
    return jax.shard_map(shards, mesh=fine, in_specs=in_specs, out_specs=out_specs, check_vma=False)
```

```python
import functools
import math

import jax
import jax.numpy as jnp
from jax import lax
from jax.experimental import pallas as pl
from jax.experimental.pallas import tpu as pltpu
from jax.sharding import Mesh, PartitionSpec as P

CAP = 2
PAD = 8
LOW = -1e30
PARTS = 4
EMPHASIS = 20
NT = (((1,), (1,)), ((), ()))


def scores_of(rows, keys):
    raw = lax.dot_general(rows, keys, NT, preferred_element_type=jnp.float32)
    return raw * (1.0 / math.sqrt(keys.shape[-1]))


def times_values(weights, values):
    return jnp.dot(weights.astype(jnp.bfloat16), values, preferred_element_type=jnp.float32)


def head_lse(lse, head, per_head, lanes):
    lse = jnp.broadcast_to(lse, (lse.shape[0], lanes))
    row = lax.broadcasted_iota(jnp.int32, lse.shape, 0)
    col = lax.broadcasted_iota(jnp.int32, lse.shape, 1)
    lse = jnp.where(col == head * per_head + row % per_head, lse, 0.0)
    return jnp.sum(lse.reshape(-1, per_head, lanes), axis=1, keepdims=True)


def tail_rows(pieces):
    shape = pieces[0].shape[:-2] + (PAD, pieces[0].shape[-1])
    row = lax.broadcasted_iota(jnp.int32, shape, len(shape) - 2)
    out = jnp.zeros(shape, jnp.float32)
    for place, piece in enumerate(pieces):
        out = jnp.where(row == place, jnp.broadcast_to(piece, shape), out)
    return out


def split_lse(lse):
    coarse = jnp.round(lse * 0.25) * 4.0
    rest = lse - coarse
    middle = jnp.round(rest * 512.0) * (1.0 / 512.0)
    return coarse, middle, rest - middle


def join_lse(tail):
    return tail[..., 0, :] + tail[..., 1, :] + tail[..., 2, :]


def local_kernel(heads, len_ref, q_ref, k_ref, v_ref, nk_ref, nv_ref, out_ref):
    rows = q_ref.shape[0]
    per_head = rows // heads
    q = q_ref[...]
    far = scores_of(q, k_ref[...])
    row = lax.broadcasted_iota(jnp.int32, far.shape, 0)
    col = lax.broadcasted_iota(jnp.int32, far.shape, 1)
    seen = (col % heads == row // per_head) & (col < len_ref[0] * heads)
    far = jnp.where(seen, far, LOW)
    near = scores_of(q, nk_ref[...])
    row = lax.broadcasted_iota(jnp.int32, near.shape, 0)
    col = lax.broadcasted_iota(jnp.int32, near.shape, 1)
    steps = near.shape[1] // heads
    step = (row % per_head) // (per_head // steps)
    seen = (col % heads == row // per_head) & (col // heads <= step)
    near = jnp.where(seen, near, LOW)
    high = jnp.maximum(
        jnp.max(far, axis=1, keepdims=True), jnp.max(near, axis=1, keepdims=True)
    )
    far = jnp.exp(far - high)
    near = jnp.exp(near - high)
    den = jnp.sum(far, axis=1, keepdims=True) + jnp.sum(near, axis=1, keepdims=True)
    num = times_values(far, v_ref[...]) + times_values(near, nv_ref[...])
    out_ref[:rows, :] = num / den
    lse = jnp.broadcast_to(high + jnp.log(den), (rows, rows))
    row = lax.broadcasted_iota(jnp.int32, (rows, rows), 0)
    col = lax.broadcasted_iota(jnp.int32, (rows, rows), 1)
    flat = jnp.sum(jnp.where(row == col, lse, 0.0), axis=0, keepdims=True)
    out_ref[rows:, :] = jnp.broadcast_to(flat, (PAD, rows))


def select_kernel(idx_ref, peer_ref, out_ref):
    out_ref[...] = jnp.broadcast_to(peer_ref[...][None], out_ref.shape)


def branch_kernel(count, q_ref, *refs):
    sources, out_ref, held, sems = refs[:count], refs[count], refs[count + 1], refs[count + 2]
    slots, lanes, dim = q_ref.shape
    heads = sources[0].shape[0]
    per_head = lanes // heads
    group = heads // PARTS

    def copies(part):
        some = pl.ds(part * group, group)
        return [
            pltpu.make_async_copy(ref.at[some], held.at[place, some], sems.at[place, part])
            for place, ref in enumerate(sources)
        ]

    for part in range(PARTS):
        for place, copy in enumerate(copies(part)):
            copy.start(priority=place % 2)
    tail = jnp.zeros((slots, 1, lanes), jnp.float32)
    for head in range(heads):
        if head % group == 0:
            for copy in copies(head // group):
                copy.wait()
        place = slice(head * per_head, (head + 1) * per_head)
        q = q_ref[:, place, :].reshape(slots * per_head, dim)
        found = []
        for block in range(0, count, 2):
            scores = scores_of(q, held[block, head])
            high = jnp.max(scores, axis=1, keepdims=True)
            weights = jnp.exp(scores - high)
            den = jnp.sum(weights, axis=1, keepdims=True)
            found.append((high, den, times_values(weights, held[block + 1, head])))
        high = functools.reduce(jnp.maximum, [f[0] for f in found])
        factors = [jnp.exp(f[0] - high) for f in found]
        den = sum(factor * f[1] for factor, f in zip(factors, found))
        num = sum(f[2] * (factor / den) for factor, f in zip(factors, found))
        out_ref[:, place, :] = num.reshape(slots, per_head, dim)
        tail = tail + head_lse(high + jnp.log(den), head, per_head, lanes)
    out_ref[:, lanes:, :] = tail_rows(split_lse(tail))


def root_kernel(q_ref, q_twin_ref, block_ref, out_ref, out_twin_ref, held, sems):
    requests, lanes, dim = q_ref.shape
    blocks, heads, half = held.shape[0], held.shape[1], held.shape[2] // 2
    per_head = lanes // heads
    group = heads // PARTS
    span = blocks * half

    def copies(part):
        some = pl.ds(part * group, group)
        cuts = [pl.ds(i * (blocks // 2), blocks // 2) for i in range(2)]
        return [
            pltpu.make_async_copy(
                block_ref.at[cut, some], held.at[cut, some], sems.at[place, part]
            )
            for place, cut in enumerate(cuts)
        ]

    for part in range(PARTS):
        for place, copy in enumerate(copies(part)):
            copy.start(priority=place)
    pairs = ((q_ref, out_ref), (q_twin_ref, out_twin_ref))
    tails = [jnp.zeros((requests, 1, lanes), jnp.float32) for _ in pairs]
    for head in range(heads):
        if head % group == 0:
            for copy in copies(head // group):
                copy.wait()
        place = slice(head * per_head, (head + 1) * per_head)
        keys = held[:, head, :half, :].reshape(span, dim)
        values = held[:, head, half:, :].reshape(span, dim)
        for i, (rows_ref, result_ref) in enumerate(pairs):
            q = rows_ref[:, place, :].reshape(requests * per_head, dim)
            scores = scores_of(q, keys)
            high = jnp.max(scores, axis=1, keepdims=True)
            weights = jnp.exp(scores - high)
            den = jnp.sum(weights, axis=1, keepdims=True)
            num = times_values(weights, values) / den
            result_ref[:, place, :] = num.reshape(requests, per_head, dim)
            tails[i] = tails[i] + head_lse(high + jnp.log(den), head, per_head, lanes)
    for (_, result_ref), tail in zip(pairs, tails):
        result_ref[:, lanes:, :] = tail_rows(split_lse(tail))


def columns(table):
    lanes = table.shape[1]
    rest = jnp.zeros((lanes - table.shape[0], lanes), jnp.float32)
    return jnp.concatenate([table, rest], axis=0).T


def merge_kernel(idx_ref, part_ref, own_ref, twin_ref, out_ref):
    sources, cap, _, lanes = part_ref.shape
    groups = own_ref.shape[0]
    lse_a = join_lse(own_ref[:, lanes:, :])
    lse_b = join_lse(twin_ref[:, lanes:, :])
    high = jnp.maximum(lse_a, lse_b)
    factor_a = jnp.exp(lse_a - high)
    factor_b = jnp.exp(lse_b - high)
    total = factor_a + factor_b
    table = columns(jnp.concatenate([factor_a / total, factor_b / total], axis=0))
    pieces = split_lse(high + jnp.log(total))
    for r in range(groups):
        out_ref[r, :lanes, :] = (
            own_ref[r, :lanes, :] * table[:, r : r + 1]
            + twin_ref[r, :lanes, :] * table[:, groups + r : groups + r + 1]
        )
        out_ref[r, lanes:, :] = tail_rows([piece[r : r + 1] for piece in pieces])
    for k in range(cap):
        reader = idx_ref[k]

        @pl.when(reader >= 0)
        def _():
            lse = join_lse(part_ref[:, k, lanes:, :])
            near = join_lse(out_ref[reader, lanes:, :])[None]
            high = jnp.maximum(jnp.max(lse, axis=0, keepdims=True), near)
            factor = jnp.exp(lse - high)
            near = jnp.exp(near - high)
            total = jnp.sum(factor, axis=0, keepdims=True) + near
            table = columns(jnp.concatenate([factor / total, near / total], axis=0))
            out = out_ref[reader, :lanes, :] * table[:, sources : sources + 1]
            for source in range(sources):
                out = out + part_ref[source, k, :lanes, :] * table[:, source : source + 1]
            out_ref[reader, :lanes, :] = out
            out_ref[reader, lanes:, :] = tail_rows(split_lse(high + jnp.log(total)))


def final_kernel(part_ref, local_ref, out_ref):
    groups, _, lanes = part_ref.shape
    lse = join_lse(part_ref[:, lanes:, :])
    near = local_ref[lanes : lanes + 1, :]
    high = jnp.maximum(jnp.max(lse, axis=0, keepdims=True), near)
    factor = jnp.exp(lse - high)
    near = jnp.exp(near - high)
    total = jnp.sum(factor, axis=0, keepdims=True) + near
    table = columns(jnp.concatenate([factor / total, near / total], axis=0))
    out = local_ref[:lanes, :] * table[:, groups : groups + 1]
    for source in range(groups):
        out = out + part_ref[source, :lanes, :] * table[:, source : source + 1]
    out_ref[...] = out.astype(out_ref.dtype)


def params(megabytes=20):
    return pltpu.CompilerParams(vmem_limit_bytes=megabytes * 1024 * 1024)


def estimate(area, dim, emphasis=1):
    return pl.CostEstimate(
        flops=emphasis * 4 * area * dim, bytes_accessed=6 * 1024 * 1024, transcendentals=area
    )


def vmem():
    return pl.BlockSpec(memory_space=pltpu.VMEM)


def hbm():
    return pl.BlockSpec(memory_space=pltpu.HBM)


def smem():
    return pl.BlockSpec(memory_space=pltpu.SMEM)


def scratch(count, shape):
    return [pltpu.VMEM(shape, jnp.bfloat16), pltpu.SemaphoreType.DMA((count, PARTS))]


def in_hbm(blocks):
    return [pltpu.with_memory_space_constraint(block, pltpu.HBM) for block in blocks]


def exchange(blocks, axis):
    return lax.all_to_all(blocks, axis, split_axis=0, concat_axis=0, tiled=True)


def to_all(block, axis):
    return exchange(jnp.broadcast_to(block[None], (lax.axis_size(axis),) + block.shape), axis)


def shards(
    queries,
    root_keys,
    root_values,
    branch_keys,
    branch_values,
    suffix_keys,
    suffix_values,
    new_keys,
    new_values,
    branch_of,
    owner,
    suffix_len,
):
    steps, q_heads, dim = queries.shape[1:]
    heads = root_keys.shape[1]
    group = q_heads // heads
    per_head = steps * group
    rows = heads * per_head
    grp = lax.axis_size("grp")
    ring = lax.axis_size("z")
    core = lax.axis_size("core")
    spots = lax.axis_size("xhi") * ring * core
    grp_place = lax.axis_index("grp")
    seq_place = (lax.axis_index("xhi") * ring + lax.axis_index("z")) * core + lax.axis_index("core")
    swap = [(0, 1), (1, 0)]

    q_rows = queries[0].reshape(steps, heads, group, dim).transpose(1, 0, 2, 3)
    q_rows = q_rows.reshape(rows, dim)
    peers = to_all(q_rows, "grp")

    matches = branch_of[:, None] == jnp.arange(owner.shape[0])[None, :]
    slot_of = jnp.sum(jnp.where(matches, owner[None, :], 0), axis=1)
    slot_here = lax.dynamic_slice_in_dim(slot_of.reshape(grp, spots), seq_place, 1, 1)[:, 0]
    reading = slot_here == grp_place
    group_ids = jnp.arange(grp)
    before = jnp.sum((reading[None, :] & (group_ids[None, :] < group_ids[:, None])), axis=1)
    chosen = reading[None, :] & (before[None, :] == jnp.arange(CAP)[:, None])
    readers = jnp.max(jnp.where(chosen, group_ids[None, :], -1), axis=1).astype(jnp.int32)

    area = ring * CAP * rows * branch_keys.shape[1] * 4

    def gather_readers(peers):
        packed = pl.pallas_call(
            select_kernel,
            out_shape=jax.ShapeDtypeStruct((ring, CAP, rows, dim), jnp.bfloat16),
            grid_spec=pltpu.PrefetchScalarGridSpec(
                num_scalar_prefetch=1,
                grid=(CAP,),
                in_specs=[
                    pl.BlockSpec((1, rows, dim), lambda k, idx: (jnp.maximum(idx[k], 0), 0, 0))
                ],
                out_specs=pl.BlockSpec((ring, 1, rows, dim), lambda k, idx: (0, k, 0, 0)),
            ),
            compiler_params=params(),
            cost_estimate=estimate(area, dim, EMPHASIS),
            name="pick_readers",
        )(readers, peers)
        return exchange(packed, "z")

    root_block = jnp.concatenate([root_keys, root_values], axis=0).transpose(1, 0, 2)
    pair = jnp.stack([root_block, lax.ppermute(root_block, "xhi", swap)])
    pair, keys_own, values_own = lax.optimization_barrier((pair, branch_keys[0], branch_values[0]))
    root_own = lax.all_gather(pair, "z", axis=0, tiled=True)
    keys_own = keys_own.transpose(1, 0, 2)
    values_own = values_own.transpose(1, 0, 2)
    peers, _ = lax.optimization_barrier((peers, pair))
    keys_far = lax.ppermute(keys_own, "xhi", swap)
    values_far = lax.ppermute(values_own, "xhi", swap)
    slots = gather_readers(peers)
    branch_blocks = [
        keys_own,
        values_own,
        lax.ppermute(keys_own, "core", swap),
        lax.ppermute(values_own, "core", swap),
        keys_far,
        values_far,
        lax.ppermute(keys_far, "core", swap),
        lax.ppermute(values_far, "core", swap),
    ]
    flat = suffix_keys.shape[1] * heads
    local = pl.pallas_call(
        functools.partial(local_kernel, heads),
        out_shape=jax.ShapeDtypeStruct((rows + PAD, dim), jnp.float32),
        in_specs=[smem()] + [vmem()] * 5,
        out_specs=vmem(),
        compiler_params=params(),
        cost_estimate=pl.CostEstimate(
            flops=4 * rows * flat * dim, bytes_accessed=4 * flat * dim, transcendentals=rows * flat
        ),
        name="local_attention",
    )(
        suffix_len,
        q_rows,
        suffix_keys.reshape(flat, dim),
        suffix_values.reshape(flat, dim),
        new_keys.reshape(steps * heads, dim),
        new_values.reshape(steps * heads, dim),
    )

    slots = slots.reshape(ring * CAP, rows, dim)
    area = ring * CAP * rows * branch_keys.shape[1] * 4
    count = len(branch_blocks)
    parts = pl.pallas_call(
        functools.partial(branch_kernel, count),
        out_shape=jax.ShapeDtypeStruct((ring * CAP, rows + PAD, dim), jnp.float32),
        in_specs=[vmem()] + [hbm()] * count,
        out_specs=vmem(),
        scratch_shapes=scratch(count, (count,) + keys_own.shape),
        compiler_params=params(),
        cost_estimate=estimate(area, dim),
        name="branch_attention",
    )(slots, *in_hbm(branch_blocks))
    parts = parts.astype(jnp.float16).reshape(ring, CAP, rows + PAD, dim)
    peers_twin = lax.ppermute(peers, "core", swap)
    peers, peers_twin, _ = lax.optimization_barrier((peers, peers_twin, parts))
    parts = exchange(parts, "z")

    whole = jax.ShapeDtypeStruct((grp, rows + PAD, dim), jnp.float32)
    root, root_twin = pl.pallas_call(
        root_kernel,
        out_shape=(whole, whole),
        in_specs=[vmem()] * 2 + [hbm()],
        out_specs=(vmem(), vmem()),
        scratch_shapes=scratch(2, root_own.shape),
        compiler_params=params(),
        cost_estimate=estimate(area, dim),
        name="root_attention",
    )(peers, peers_twin, *in_hbm([root_own]))
    root_twin = lax.ppermute(root_twin.astype(jnp.float16), "core", swap).astype(jnp.float32)
    parts, root, root_twin = lax.optimization_barrier((parts, root, root_twin))
    parts = parts.astype(jnp.float32)
    merged = pl.pallas_call(
        merge_kernel,
        out_shape=whole,
        in_specs=[smem()] + [vmem()] * 3,
        out_specs=vmem(),
        compiler_params=params(),
        name="merge_parts",
    )(readers, parts, root, root_twin)
    back = exchange(merged.astype(jnp.float16), "grp").astype(jnp.float32)
    mine = pl.pallas_call(
        final_kernel,
        out_shape=jax.ShapeDtypeStruct((rows, dim), jnp.bfloat16),
        in_specs=[vmem()] * 2,
        out_specs=vmem(),
        compiler_params=params(),
        name="final_merge",
    )(back, local)
    mine = mine.reshape(heads, steps, group, dim).transpose(1, 0, 2, 3)
    return mine.reshape(queries.shape)


def solution(mesh):
    grp, seq = mesh.devices.shape
    fine = Mesh(mesh.devices.reshape(grp, 2, seq // 4, 2), ("grp", "xhi", "z", "core"))
    seq = ("xhi", "z", "core")
    both = ("grp",) + seq
    in_specs = (
        P(both, None, None, None),
        P(both, None, None),
        P(both, None, None),
        P("grp", seq, None, None),
        P("grp", seq, None, None),
        P(both, None, None, None),
        P(both, None, None, None),
        P(both, None, None, None),
        P(both, None, None, None),
        P(),
        P(),
        P(both),
    )
    out_specs = P(both, None, None, None)
    return jax.shard_map(shards, mesh=fine, in_specs=in_specs, out_specs=out_specs, check_vma=False)
```

```python
import functools
import math

import jax
import jax.numpy as jnp
from jax import lax
from jax.experimental import pallas as pl
from jax.experimental.pallas import tpu as pltpu
from jax.sharding import Mesh, PartitionSpec as P

CAP = 2
PAD = 8
LOW = -1e30
PARTS = 8
EMPHASIS = 20
NT = (((1,), (1,)), ((), ()))


def scores_of(rows, keys):
    raw = lax.dot_general(rows, keys, NT, preferred_element_type=jnp.float32)
    return raw * (1.0 / math.sqrt(keys.shape[-1]))


def times_values(weights, values):
    return jnp.dot(weights.astype(jnp.bfloat16), values, preferred_element_type=jnp.float32)


def head_lse(lse, head, per_head, lanes):
    lse = jnp.broadcast_to(lse, (lse.shape[0], lanes))
    row = lax.broadcasted_iota(jnp.int32, lse.shape, 0)
    col = lax.broadcasted_iota(jnp.int32, lse.shape, 1)
    lse = jnp.where(col == head * per_head + row % per_head, lse, 0.0)
    return jnp.sum(lse.reshape(-1, per_head, lanes), axis=1, keepdims=True)


def tail_rows(pieces):
    shape = pieces[0].shape[:-2] + (PAD, pieces[0].shape[-1])
    row = lax.broadcasted_iota(jnp.int32, shape, len(shape) - 2)
    out = jnp.zeros(shape, jnp.float32)
    for place, piece in enumerate(pieces):
        out = jnp.where(row == place, jnp.broadcast_to(piece, shape), out)
    return out


def split_lse(lse):
    coarse = jnp.round(lse * 0.25) * 4.0
    rest = lse - coarse
    middle = jnp.round(rest * 512.0) * (1.0 / 512.0)
    return coarse, middle, rest - middle


def join_lse(tail):
    return tail[..., 0, :] + tail[..., 1, :] + tail[..., 2, :]


def local_kernel(heads, len_ref, q_ref, k_ref, v_ref, nk_ref, nv_ref, out_ref):
    rows = q_ref.shape[0]
    per_head = rows // heads
    q = q_ref[...]
    far = scores_of(q, k_ref[...])
    row = lax.broadcasted_iota(jnp.int32, far.shape, 0)
    col = lax.broadcasted_iota(jnp.int32, far.shape, 1)
    seen = (col % heads == row // per_head) & (col < len_ref[0] * heads)
    far = jnp.where(seen, far, LOW)
    near = scores_of(q, nk_ref[...])
    row = lax.broadcasted_iota(jnp.int32, near.shape, 0)
    col = lax.broadcasted_iota(jnp.int32, near.shape, 1)
    steps = near.shape[1] // heads
    step = (row % per_head) // (per_head // steps)
    seen = (col % heads == row // per_head) & (col // heads <= step)
    near = jnp.where(seen, near, LOW)
    high = jnp.maximum(
        jnp.max(far, axis=1, keepdims=True), jnp.max(near, axis=1, keepdims=True)
    )
    far = jnp.exp(far - high)
    near = jnp.exp(near - high)
    den = jnp.sum(far, axis=1, keepdims=True) + jnp.sum(near, axis=1, keepdims=True)
    num = times_values(far, v_ref[...]) + times_values(near, nv_ref[...])
    out_ref[:rows, :] = num / den
    lse = jnp.broadcast_to(high + jnp.log(den), (rows, rows))
    row = lax.broadcasted_iota(jnp.int32, (rows, rows), 0)
    col = lax.broadcasted_iota(jnp.int32, (rows, rows), 1)
    flat = jnp.sum(jnp.where(row == col, lse, 0.0), axis=0, keepdims=True)
    out_ref[rows:, :] = jnp.broadcast_to(flat, (PAD, rows))


def order_kernel(heads, q_ref, copies_ref, rows_ref):
    steps, q_heads, _ = q_ref.shape
    group = q_heads // heads
    q = q_ref[...].astype(jnp.float32)
    rows = [q[t, j * group : (j + 1) * group] for j in range(heads) for t in range(steps)]
    rows = jnp.concatenate(rows, axis=0).astype(rows_ref.dtype)
    rows_ref[...] = rows
    copies_ref[...] = jnp.broadcast_to(rows[None], copies_ref.shape)


def select_kernel(idx_ref, peer_ref, out_ref):
    out_ref[...] = jnp.broadcast_to(peer_ref[...][None], out_ref.shape)


def branch_kernel(count, q_ref, *refs):
    sources, out_ref, held, sems = refs[:count], refs[count], refs[count + 1], refs[count + 2]
    slots, lanes, dim = q_ref.shape
    heads = sources[0].shape[0]
    per_head = lanes // heads
    group = heads // PARTS

    def copies(part):
        some = pl.ds(part * group, group)
        return [
            pltpu.make_async_copy(ref.at[some], held.at[place, some], sems.at[place, part])
            for place, ref in enumerate(sources)
        ]

    for part in range(PARTS):
        for place, copy in enumerate(copies(part)):
            copy.start(priority=place % 2)
    tail = jnp.zeros((slots, 1, lanes), jnp.float32)
    for head in range(heads):
        if head % group == 0:
            for copy in copies(head // group):
                copy.wait()
        place = slice(head * per_head, (head + 1) * per_head)
        q = q_ref[:, place, :].reshape(slots * per_head, dim)
        found = []
        for block in range(0, count, 2):
            scores = scores_of(q, held[block, head])
            high = jnp.max(scores, axis=1, keepdims=True)
            weights = jnp.exp(scores - high)
            den = jnp.sum(weights, axis=1, keepdims=True)
            found.append((high, den, times_values(weights, held[block + 1, head])))
        high = functools.reduce(jnp.maximum, [f[0] for f in found])
        factors = [jnp.exp(f[0] - high) for f in found]
        den = sum(factor * f[1] for factor, f in zip(factors, found))
        num = sum(f[2] * (factor / den) for factor, f in zip(factors, found))
        out_ref[:, place, :] = num.reshape(slots, per_head, dim)
        tail = tail + head_lse(high + jnp.log(den), head, per_head, lanes)
    out_ref[:, lanes:, :] = tail_rows(split_lse(tail))


def root_kernel(q_ref, q_twin_ref, block_ref, out_ref, out_twin_ref, held, sems):
    requests, lanes, dim = q_ref.shape
    blocks, heads, half = held.shape[0], held.shape[1], held.shape[2] // 2
    per_head = lanes // heads
    group = heads // PARTS
    span = blocks * half

    def copies(part):
        some = pl.ds(part * group, group)
        cuts = [pl.ds(i * (blocks // 2), blocks // 2) for i in range(2)]
        return [
            pltpu.make_async_copy(
                block_ref.at[cut, some], held.at[cut, some], sems.at[place, part]
            )
            for place, cut in enumerate(cuts)
        ]

    for part in range(PARTS):
        for place, copy in enumerate(copies(part)):
            copy.start(priority=place)
    pairs = ((q_ref, out_ref), (q_twin_ref, out_twin_ref))
    tails = [jnp.zeros((requests, 1, lanes), jnp.float32) for _ in pairs]
    for head in range(heads):
        if head % group == 0:
            for copy in copies(head // group):
                copy.wait()
        place = slice(head * per_head, (head + 1) * per_head)
        keys = held[:, head, :half, :].reshape(span, dim)
        values = held[:, head, half:, :].reshape(span, dim)
        for i, (rows_ref, result_ref) in enumerate(pairs):
            q = rows_ref[:, place, :].reshape(requests * per_head, dim)
            scores = scores_of(q, keys)
            high = jnp.max(scores, axis=1, keepdims=True)
            weights = jnp.exp(scores - high)
            den = jnp.sum(weights, axis=1, keepdims=True)
            num = times_values(weights, values) / den
            result_ref[:, place, :] = num.reshape(requests, per_head, dim)
            tails[i] = tails[i] + head_lse(high + jnp.log(den), head, per_head, lanes)
    for (_, result_ref), tail in zip(pairs, tails):
        result_ref[:, lanes:, :] = tail_rows(split_lse(tail))


def columns(table):
    lanes = table.shape[1]
    rest = jnp.zeros((lanes - table.shape[0], lanes), jnp.float32)
    return jnp.concatenate([table, rest], axis=0).T


def merge_kernel(idx_ref, part_ref, own_ref, twin_ref, out_ref):
    sources, cap, _, lanes = part_ref.shape
    groups = own_ref.shape[0]
    lse_a = join_lse(own_ref[:, lanes:, :])
    lse_b = join_lse(twin_ref[:, lanes:, :])
    high = jnp.maximum(lse_a, lse_b)
    factor_a = jnp.exp(lse_a - high)
    factor_b = jnp.exp(lse_b - high)
    total = factor_a + factor_b
    table = columns(jnp.concatenate([factor_a / total, factor_b / total], axis=0))
    pieces = split_lse(high + jnp.log(total))
    for r in range(groups):
        out_ref[r, :lanes, :] = (
            own_ref[r, :lanes, :] * table[:, r : r + 1]
            + twin_ref[r, :lanes, :] * table[:, groups + r : groups + r + 1]
        )
        out_ref[r, lanes:, :] = tail_rows([piece[r : r + 1] for piece in pieces])
    for k in range(cap):
        reader = idx_ref[k]

        @pl.when(reader >= 0)
        def _():
            lse = join_lse(part_ref[:, k, lanes:, :])
            near = join_lse(out_ref[reader, lanes:, :])[None]
            high = jnp.maximum(jnp.max(lse, axis=0, keepdims=True), near)
            factor = jnp.exp(lse - high)
            near = jnp.exp(near - high)
            total = jnp.sum(factor, axis=0, keepdims=True) + near
            table = columns(jnp.concatenate([factor / total, near / total], axis=0))
            out = out_ref[reader, :lanes, :] * table[:, sources : sources + 1]
            for source in range(sources):
                out = out + part_ref[source, k, :lanes, :] * table[:, source : source + 1]
            out_ref[reader, :lanes, :] = out
            out_ref[reader, lanes:, :] = tail_rows(split_lse(high + jnp.log(total)))


def final_kernel(heads, part_ref, local_ref, out_ref):
    groups, _, lanes = part_ref.shape
    lse = join_lse(part_ref[:, lanes:, :])
    near = local_ref[lanes : lanes + 1, :]
    high = jnp.maximum(jnp.max(lse, axis=0, keepdims=True), near)
    factor = jnp.exp(lse - high)
    near = jnp.exp(near - high)
    total = jnp.sum(factor, axis=0, keepdims=True) + near
    table = columns(jnp.concatenate([factor / total, near / total], axis=0))
    out = local_ref[:lanes, :] * table[:, groups : groups + 1]
    for source in range(groups):
        out = out + part_ref[source, :lanes, :] * table[:, source : source + 1]
    steps, q_heads, _ = out_ref.shape
    group = q_heads // heads
    for t in range(steps):
        starts = [(j * steps + t) * group for j in range(heads)]
        rows = jnp.concatenate([out[start : start + group] for start in starts], axis=0)
        out_ref[t] = rows.astype(out_ref.dtype)


def params(megabytes=20):
    return pltpu.CompilerParams(vmem_limit_bytes=megabytes * 1024 * 1024)


def estimate(area, dim, emphasis=1):
    return pl.CostEstimate(
        flops=emphasis * 4 * area * dim, bytes_accessed=6 * 1024 * 1024, transcendentals=area
    )


def vmem():
    return pl.BlockSpec(memory_space=pltpu.VMEM)


def hbm():
    return pl.BlockSpec(memory_space=pltpu.HBM)


def smem():
    return pl.BlockSpec(memory_space=pltpu.SMEM)


def scratch(count, shape):
    return [pltpu.VMEM(shape, jnp.bfloat16), pltpu.SemaphoreType.DMA((count, PARTS))]


def in_hbm(blocks):
    return [pltpu.with_memory_space_constraint(block, pltpu.HBM) for block in blocks]


def exchange(blocks, axis):
    return lax.all_to_all(blocks, axis, split_axis=0, concat_axis=0, tiled=True)


def shards(
    queries,
    root_keys,
    root_values,
    branch_keys,
    branch_values,
    suffix_keys,
    suffix_values,
    new_keys,
    new_values,
    branch_of,
    owner,
    suffix_len,
):
    steps, q_heads, dim = queries.shape[1:]
    heads = root_keys.shape[1]
    group = q_heads // heads
    per_head = steps * group
    rows = heads * per_head
    grp = lax.axis_size("grp")
    ring = lax.axis_size("z")
    core = lax.axis_size("core")
    spots = lax.axis_size("xhi") * ring * core
    grp_place = lax.axis_index("grp")
    seq_place = (lax.axis_index("xhi") * ring + lax.axis_index("z")) * core + lax.axis_index("core")
    swap = [(0, 1), (1, 0)]

    copies, q_rows = pl.pallas_call(
        functools.partial(order_kernel, heads),
        out_shape=(
            jax.ShapeDtypeStruct((grp, rows, dim), jnp.bfloat16),
            jax.ShapeDtypeStruct((rows, dim), jnp.bfloat16),
        ),
        in_specs=[vmem()],
        out_specs=(vmem(), vmem()),
        compiler_params=params(),
        name="order_queries",
    )(queries[0])
    peers = exchange(copies, "grp")

    matches = branch_of[:, None] == jnp.arange(owner.shape[0])[None, :]
    slot_of = jnp.sum(jnp.where(matches, owner[None, :], 0), axis=1)
    slot_here = lax.dynamic_slice_in_dim(slot_of.reshape(grp, spots), seq_place, 1, 1)[:, 0]
    reading = slot_here == grp_place
    group_ids = jnp.arange(grp)
    before = jnp.sum((reading[None, :] & (group_ids[None, :] < group_ids[:, None])), axis=1)
    chosen = reading[None, :] & (before[None, :] == jnp.arange(CAP)[:, None])
    readers = jnp.max(jnp.where(chosen, group_ids[None, :], -1), axis=1).astype(jnp.int32)

    area = ring * CAP * rows * branch_keys.shape[1] * 4

    def gather_readers(peers):
        packed = pl.pallas_call(
            select_kernel,
            out_shape=jax.ShapeDtypeStruct((ring, CAP, rows, dim), jnp.bfloat16),
            grid_spec=pltpu.PrefetchScalarGridSpec(
                num_scalar_prefetch=1,
                grid=(CAP,),
                in_specs=[
                    pl.BlockSpec((1, rows, dim), lambda k, idx: (jnp.maximum(idx[k], 0), 0, 0))
                ],
                out_specs=pl.BlockSpec((ring, 1, rows, dim), lambda k, idx: (0, k, 0, 0)),
            ),
            compiler_params=params(),
            cost_estimate=estimate(area, dim, EMPHASIS),
            name="pick_readers",
        )(readers, peers)
        return exchange(packed, "z")

    root_block = jnp.concatenate([root_keys, root_values], axis=0).transpose(1, 0, 2)
    pair = jnp.stack([root_block, lax.ppermute(root_block, "xhi", swap)])
    pair, keys_own, values_own = lax.optimization_barrier((pair, branch_keys[0], branch_values[0]))
    root_own = lax.all_gather(pair, "z", axis=0, tiled=True)
    keys_own = keys_own.transpose(1, 0, 2)
    values_own = values_own.transpose(1, 0, 2)
    peers, _ = lax.optimization_barrier((peers, pair))
    keys_far = lax.ppermute(keys_own, "xhi", swap)
    values_far = lax.ppermute(values_own, "xhi", swap)
    slots = gather_readers(peers)
    branch_blocks = [
        keys_own,
        values_own,
        lax.ppermute(keys_own, "core", swap),
        lax.ppermute(values_own, "core", swap),
        keys_far,
        values_far,
        lax.ppermute(keys_far, "core", swap),
        lax.ppermute(values_far, "core", swap),
    ]
    flat = suffix_keys.shape[1] * heads
    local = pl.pallas_call(
        functools.partial(local_kernel, heads),
        out_shape=jax.ShapeDtypeStruct((rows + PAD, dim), jnp.float32),
        in_specs=[smem()] + [vmem()] * 5,
        out_specs=vmem(),
        compiler_params=params(),
        cost_estimate=pl.CostEstimate(
            flops=4 * rows * flat * dim, bytes_accessed=4 * flat * dim, transcendentals=rows * flat
        ),
        name="local_attention",
    )(
        suffix_len,
        q_rows,
        suffix_keys.reshape(flat, dim),
        suffix_values.reshape(flat, dim),
        new_keys.reshape(steps * heads, dim),
        new_values.reshape(steps * heads, dim),
    )

    slots = slots.reshape(ring * CAP, rows, dim)
    area = ring * CAP * rows * branch_keys.shape[1] * 4
    count = len(branch_blocks)
    parts = pl.pallas_call(
        functools.partial(branch_kernel, count),
        out_shape=jax.ShapeDtypeStruct((ring * CAP, rows + PAD, dim), jnp.float32),
        in_specs=[vmem()] + [hbm()] * count,
        out_specs=vmem(),
        scratch_shapes=scratch(count, (count,) + keys_own.shape),
        compiler_params=params(),
        cost_estimate=estimate(area, dim),
        name="branch_attention",
    )(slots, *in_hbm(branch_blocks))
    parts = parts.astype(jnp.float16).reshape(ring, CAP, rows + PAD, dim)
    peers_twin = lax.ppermute(peers, "core", swap)
    peers, peers_twin, _ = lax.optimization_barrier((peers, peers_twin, parts))
    parts = exchange(parts, "z")

    whole = jax.ShapeDtypeStruct((grp, rows + PAD, dim), jnp.float32)
    root, root_twin = pl.pallas_call(
        root_kernel,
        out_shape=(whole, whole),
        in_specs=[vmem()] * 2 + [hbm()],
        out_specs=(vmem(), vmem()),
        scratch_shapes=scratch(2, root_own.shape),
        compiler_params=params(),
        cost_estimate=estimate(area, dim),
        name="root_attention",
    )(peers, peers_twin, *in_hbm([root_own]))
    root_twin = lax.ppermute(root_twin.astype(jnp.float16), "core", swap).astype(jnp.float32)
    parts, root, root_twin = lax.optimization_barrier((parts, root, root_twin))
    parts = parts.astype(jnp.float32)
    merged = pl.pallas_call(
        merge_kernel,
        out_shape=whole,
        in_specs=[smem()] + [vmem()] * 3,
        out_specs=vmem(),
        compiler_params=params(),
        name="merge_parts",
    )(readers, parts, root, root_twin)
    back = exchange(merged.astype(jnp.float16), "grp").astype(jnp.float32)
    mine = pl.pallas_call(
        functools.partial(final_kernel, heads),
        out_shape=jax.ShapeDtypeStruct((steps, q_heads, dim), jnp.bfloat16),
        in_specs=[vmem()] * 2,
        out_specs=vmem(),
        compiler_params=params(),
        name="final_merge",
    )(back, local)
    return mine.reshape(queries.shape)


def solution(mesh):
    grp, seq = mesh.devices.shape
    fine = Mesh(mesh.devices.reshape(grp, 2, seq // 4, 2), ("grp", "xhi", "z", "core"))
    seq = ("xhi", "z", "core")
    both = ("grp",) + seq
    in_specs = (
        P(both, None, None, None),
        P(both, None, None),
        P(both, None, None),
        P("grp", seq, None, None),
        P("grp", seq, None, None),
        P(both, None, None, None),
        P(both, None, None, None),
        P(both, None, None, None),
        P(both, None, None, None),
        P(),
        P(),
        P(both),
    )
    out_specs = P(both, None, None, None)
    return jax.shard_map(shards, mesh=fine, in_specs=in_specs, out_specs=out_specs, check_vma=False)
```

```python
import functools
import math

import jax
import jax.numpy as jnp
from jax import lax
from jax.experimental import pallas as pl
from jax.experimental.pallas import tpu as pltpu
from jax.sharding import Mesh, PartitionSpec as P

CAP = 2
PAD = 8
LOW = -1e30
PARTS = 2
EMPHASIS = 20
NT = (((1,), (1,)), ((), ()))


def scores_of(rows, keys):
    raw = lax.dot_general(rows, keys, NT, preferred_element_type=jnp.float32)
    return raw * (1.0 / math.sqrt(keys.shape[-1]))


def times_values(weights, values):
    return jnp.dot(weights.astype(jnp.bfloat16), values, preferred_element_type=jnp.float32)


def head_lse(lse, head, per_head, lanes):
    lse = jnp.broadcast_to(lse, (lse.shape[0], lanes))
    row = lax.broadcasted_iota(jnp.int32, lse.shape, 0)
    col = lax.broadcasted_iota(jnp.int32, lse.shape, 1)
    lse = jnp.where(col == head * per_head + row % per_head, lse, 0.0)
    return jnp.sum(lse.reshape(-1, per_head, lanes), axis=1, keepdims=True)


def tail_rows(pieces):
    shape = pieces[0].shape[:-2] + (PAD, pieces[0].shape[-1])
    row = lax.broadcasted_iota(jnp.int32, shape, len(shape) - 2)
    out = jnp.zeros(shape, jnp.float32)
    for place, piece in enumerate(pieces):
        out = jnp.where(row == place, jnp.broadcast_to(piece, shape), out)
    return out


def split_lse(lse):
    coarse = jnp.round(lse * 0.25) * 4.0
    rest = lse - coarse
    middle = jnp.round(rest * 512.0) * (1.0 / 512.0)
    return coarse, middle, rest - middle


def join_lse(tail):
    return tail[..., 0, :] + tail[..., 1, :] + tail[..., 2, :]


def local_kernel(heads, len_ref, q_ref, k_ref, v_ref, nk_ref, nv_ref, out_ref):
    rows = q_ref.shape[0]
    per_head = rows // heads
    q = q_ref[...]
    far = scores_of(q, k_ref[...])
    row = lax.broadcasted_iota(jnp.int32, far.shape, 0)
    col = lax.broadcasted_iota(jnp.int32, far.shape, 1)
    seen = (col % heads == row // per_head) & (col < len_ref[0] * heads)
    far = jnp.where(seen, far, LOW)
    near = scores_of(q, nk_ref[...])
    row = lax.broadcasted_iota(jnp.int32, near.shape, 0)
    col = lax.broadcasted_iota(jnp.int32, near.shape, 1)
    steps = near.shape[1] // heads
    step = (row % per_head) // (per_head // steps)
    seen = (col % heads == row // per_head) & (col // heads <= step)
    near = jnp.where(seen, near, LOW)
    high = jnp.maximum(
        jnp.max(far, axis=1, keepdims=True), jnp.max(near, axis=1, keepdims=True)
    )
    far = jnp.exp(far - high)
    near = jnp.exp(near - high)
    den = jnp.sum(far, axis=1, keepdims=True) + jnp.sum(near, axis=1, keepdims=True)
    num = times_values(far, v_ref[...]) + times_values(near, nv_ref[...])
    out_ref[:rows, :] = num / den
    lse = jnp.broadcast_to(high + jnp.log(den), (rows, rows))
    row = lax.broadcasted_iota(jnp.int32, (rows, rows), 0)
    col = lax.broadcasted_iota(jnp.int32, (rows, rows), 1)
    flat = jnp.sum(jnp.where(row == col, lse, 0.0), axis=0, keepdims=True)
    out_ref[rows:, :] = jnp.broadcast_to(flat, (PAD, rows))


def select_kernel(idx_ref, peer_ref, out_ref):
    out_ref[...] = jnp.broadcast_to(peer_ref[...][None], out_ref.shape)


def branch_kernel(count, q_ref, *refs):
    sources, out_ref, held, sems = refs[:count], refs[count], refs[count + 1], refs[count + 2]
    slots, lanes, dim = q_ref.shape
    heads = sources[0].shape[0]
    per_head = lanes // heads
    group = heads // PARTS

    def copies(part):
        some = pl.ds(part * group, group)
        return [
            pltpu.make_async_copy(ref.at[some], held.at[place, some], sems.at[place, part])
            for place, ref in enumerate(sources)
        ]

    for part in range(PARTS):
        for place, copy in enumerate(copies(part)):
            copy.start(priority=place % 2)
    tail = jnp.zeros((slots, 1, lanes), jnp.float32)
    for head in range(heads):
        if head % group == 0:
            for copy in copies(head // group):
                copy.wait()
        place = slice(head * per_head, (head + 1) * per_head)
        q = q_ref[:, place, :].reshape(slots * per_head, dim)
        found = []
        for block in range(0, count, 2):
            scores = scores_of(q, held[block, head])
            high = jnp.max(scores, axis=1, keepdims=True)
            weights = jnp.exp(scores - high)
            den = jnp.sum(weights, axis=1, keepdims=True)
            found.append((high, den, times_values(weights, held[block + 1, head])))
        high = functools.reduce(jnp.maximum, [f[0] for f in found])
        factors = [jnp.exp(f[0] - high) for f in found]
        den = sum(factor * f[1] for factor, f in zip(factors, found))
        num = sum(f[2] * (factor / den) for factor, f in zip(factors, found))
        out_ref[:, place, :] = num.reshape(slots, per_head, dim)
        tail = tail + head_lse(high + jnp.log(den), head, per_head, lanes)
    out_ref[:, lanes:, :] = tail_rows(split_lse(tail))


def root_kernel(q_ref, q_twin_ref, block_ref, out_ref, out_twin_ref, held, sems):
    requests, lanes, dim = q_ref.shape
    blocks, heads, half = held.shape[0], held.shape[1], held.shape[2] // 2
    per_head = lanes // heads
    group = heads // PARTS
    span = blocks * half

    def copies(part):
        some = pl.ds(part * group, group)
        cuts = [pl.ds(i * (blocks // 2), blocks // 2) for i in range(2)]
        return [
            pltpu.make_async_copy(
                block_ref.at[cut, some], held.at[cut, some], sems.at[place, part]
            )
            for place, cut in enumerate(cuts)
        ]

    for part in range(PARTS):
        for place, copy in enumerate(copies(part)):
            copy.start(priority=place)
    pairs = ((q_ref, out_ref), (q_twin_ref, out_twin_ref))
    tails = [jnp.zeros((requests, 1, lanes), jnp.float32) for _ in pairs]
    for head in range(heads):
        if head % group == 0:
            for copy in copies(head // group):
                copy.wait()
        place = slice(head * per_head, (head + 1) * per_head)
        keys = held[:, head, :half, :].reshape(span, dim)
        values = held[:, head, half:, :].reshape(span, dim)
        for i, (rows_ref, result_ref) in enumerate(pairs):
            q = rows_ref[:, place, :].reshape(requests * per_head, dim)
            scores = scores_of(q, keys)
            high = jnp.max(scores, axis=1, keepdims=True)
            weights = jnp.exp(scores - high)
            den = jnp.sum(weights, axis=1, keepdims=True)
            num = times_values(weights, values) / den
            result_ref[:, place, :] = num.reshape(requests, per_head, dim)
            tails[i] = tails[i] + head_lse(high + jnp.log(den), head, per_head, lanes)
    for (_, result_ref), tail in zip(pairs, tails):
        result_ref[:, lanes:, :] = tail_rows(split_lse(tail))


def columns(table):
    lanes = table.shape[1]
    rest = jnp.zeros((lanes - table.shape[0], lanes), jnp.float32)
    return jnp.concatenate([table, rest], axis=0).T


def merge_kernel(idx_ref, part_ref, own_ref, twin_ref, out_ref):
    sources, cap, _, lanes = part_ref.shape
    groups = own_ref.shape[0]
    lse_a = join_lse(own_ref[:, lanes:, :])
    lse_b = join_lse(twin_ref[:, lanes:, :])
    high = jnp.maximum(lse_a, lse_b)
    factor_a = jnp.exp(lse_a - high)
    factor_b = jnp.exp(lse_b - high)
    total = factor_a + factor_b
    table = columns(jnp.concatenate([factor_a / total, factor_b / total], axis=0))
    pieces = split_lse(high + jnp.log(total))
    for r in range(groups):
        out_ref[r, :lanes, :] = (
            own_ref[r, :lanes, :] * table[:, r : r + 1]
            + twin_ref[r, :lanes, :] * table[:, groups + r : groups + r + 1]
        )
        out_ref[r, lanes:, :] = tail_rows([piece[r : r + 1] for piece in pieces])
    for k in range(cap):
        reader = idx_ref[k]

        @pl.when(reader >= 0)
        def _():
            lse = join_lse(part_ref[:, k, lanes:, :])
            near = join_lse(out_ref[reader, lanes:, :])[None]
            high = jnp.maximum(jnp.max(lse, axis=0, keepdims=True), near)
            factor = jnp.exp(lse - high)
            near = jnp.exp(near - high)
            total = jnp.sum(factor, axis=0, keepdims=True) + near
            table = columns(jnp.concatenate([factor / total, near / total], axis=0))
            out = out_ref[reader, :lanes, :] * table[:, sources : sources + 1]
            for source in range(sources):
                out = out + part_ref[source, k, :lanes, :] * table[:, source : source + 1]
            out_ref[reader, :lanes, :] = out
            out_ref[reader, lanes:, :] = tail_rows(split_lse(high + jnp.log(total)))


def final_kernel(part_ref, local_ref, out_ref):
    groups, _, lanes = part_ref.shape
    lse = join_lse(part_ref[:, lanes:, :])
    near = local_ref[lanes : lanes + 1, :]
    high = jnp.maximum(jnp.max(lse, axis=0, keepdims=True), near)
    factor = jnp.exp(lse - high)
    near = jnp.exp(near - high)
    total = jnp.sum(factor, axis=0, keepdims=True) + near
    table = columns(jnp.concatenate([factor / total, near / total], axis=0))
    out = local_ref[:lanes, :] * table[:, groups : groups + 1]
    for source in range(groups):
        out = out + part_ref[source, :lanes, :] * table[:, source : source + 1]
    out_ref[...] = out.astype(out_ref.dtype)


def params(megabytes=20):
    return pltpu.CompilerParams(vmem_limit_bytes=megabytes * 1024 * 1024)


def estimate(area, dim, emphasis=1):
    return pl.CostEstimate(
        flops=emphasis * 4 * area * dim, bytes_accessed=6 * 1024 * 1024, transcendentals=area
    )


def vmem():
    return pl.BlockSpec(memory_space=pltpu.VMEM)


def hbm():
    return pl.BlockSpec(memory_space=pltpu.HBM)


def smem():
    return pl.BlockSpec(memory_space=pltpu.SMEM)


def scratch(count, shape):
    return [pltpu.VMEM(shape, jnp.bfloat16), pltpu.SemaphoreType.DMA((count, PARTS))]


def in_hbm(blocks):
    return [pltpu.with_memory_space_constraint(block, pltpu.HBM) for block in blocks]


def exchange(blocks, axis):
    return lax.all_to_all(blocks, axis, split_axis=0, concat_axis=0, tiled=True)


def to_all(block, axis):
    return exchange(jnp.broadcast_to(block[None], (lax.axis_size(axis),) + block.shape), axis)


def shards(
    queries,
    root_keys,
    root_values,
    branch_keys,
    branch_values,
    suffix_keys,
    suffix_values,
    new_keys,
    new_values,
    branch_of,
    owner,
    suffix_len,
):
    steps, q_heads, dim = queries.shape[1:]
    heads = root_keys.shape[1]
    group = q_heads // heads
    per_head = steps * group
    rows = heads * per_head
    grp = lax.axis_size("grp")
    ring = lax.axis_size("z")
    core = lax.axis_size("core")
    spots = lax.axis_size("xhi") * ring * core
    grp_place = lax.axis_index("grp")
    seq_place = (lax.axis_index("xhi") * ring + lax.axis_index("z")) * core + lax.axis_index("core")
    swap = [(0, 1), (1, 0)]

    q_rows = queries[0].reshape(steps, heads, group, dim).transpose(1, 0, 2, 3)
    q_rows = q_rows.reshape(rows, dim)
    peers = to_all(q_rows, "grp")

    matches = branch_of[:, None] == jnp.arange(owner.shape[0])[None, :]
    slot_of = jnp.sum(jnp.where(matches, owner[None, :], 0), axis=1)
    slot_here = lax.dynamic_slice_in_dim(slot_of.reshape(grp, spots), seq_place, 1, 1)[:, 0]
    reading = slot_here == grp_place
    group_ids = jnp.arange(grp)
    before = jnp.sum((reading[None, :] & (group_ids[None, :] < group_ids[:, None])), axis=1)
    chosen = reading[None, :] & (before[None, :] == jnp.arange(CAP)[:, None])
    readers = jnp.max(jnp.where(chosen, group_ids[None, :], -1), axis=1).astype(jnp.int32)

    area = ring * CAP * rows * branch_keys.shape[1] * 4

    def gather_readers(peers):
        packed = pl.pallas_call(
            select_kernel,
            out_shape=jax.ShapeDtypeStruct((ring, CAP, rows, dim), jnp.bfloat16),
            grid_spec=pltpu.PrefetchScalarGridSpec(
                num_scalar_prefetch=1,
                grid=(CAP,),
                in_specs=[
                    pl.BlockSpec((1, rows, dim), lambda k, idx: (jnp.maximum(idx[k], 0), 0, 0))
                ],
                out_specs=pl.BlockSpec((ring, 1, rows, dim), lambda k, idx: (0, k, 0, 0)),
            ),
            compiler_params=params(),
            cost_estimate=estimate(area, dim, EMPHASIS),
            name="pick_readers",
        )(readers, peers)
        return exchange(packed, "z")

    root_block = jnp.concatenate([root_keys, root_values], axis=0).transpose(1, 0, 2)
    pair = jnp.stack([root_block, lax.ppermute(root_block, "xhi", swap)])
    pair, keys_own, values_own = lax.optimization_barrier((pair, branch_keys[0], branch_values[0]))
    root_own = lax.all_gather(pair, "z", axis=0, tiled=True)
    keys_own = keys_own.transpose(1, 0, 2)
    values_own = values_own.transpose(1, 0, 2)
    peers, _ = lax.optimization_barrier((peers, pair))
    keys_far = lax.ppermute(keys_own, "xhi", swap)
    values_far = lax.ppermute(values_own, "xhi", swap)
    slots = gather_readers(peers)
    branch_blocks = [
        keys_own,
        values_own,
        lax.ppermute(keys_own, "core", swap),
        lax.ppermute(values_own, "core", swap),
        keys_far,
        values_far,
        lax.ppermute(keys_far, "core", swap),
        lax.ppermute(values_far, "core", swap),
    ]
    flat = suffix_keys.shape[1] * heads
    local = pl.pallas_call(
        functools.partial(local_kernel, heads),
        out_shape=jax.ShapeDtypeStruct((rows + PAD, dim), jnp.float32),
        in_specs=[smem()] + [vmem()] * 5,
        out_specs=vmem(),
        compiler_params=params(),
        cost_estimate=pl.CostEstimate(
            flops=4 * rows * flat * dim, bytes_accessed=4 * flat * dim, transcendentals=rows * flat
        ),
        name="local_attention",
    )(
        suffix_len,
        q_rows,
        suffix_keys.reshape(flat, dim),
        suffix_values.reshape(flat, dim),
        new_keys.reshape(steps * heads, dim),
        new_values.reshape(steps * heads, dim),
    )

    slots = slots.reshape(ring * CAP, rows, dim)
    area = ring * CAP * rows * branch_keys.shape[1] * 4
    count = len(branch_blocks)
    parts = pl.pallas_call(
        functools.partial(branch_kernel, count),
        out_shape=jax.ShapeDtypeStruct((ring * CAP, rows + PAD, dim), jnp.float32),
        in_specs=[vmem()] + [hbm()] * count,
        out_specs=vmem(),
        scratch_shapes=scratch(count, (count,) + keys_own.shape),
        compiler_params=params(),
        cost_estimate=estimate(area, dim),
        name="branch_attention",
    )(slots, *in_hbm(branch_blocks))
    parts = parts.astype(jnp.float16).reshape(ring, CAP, rows + PAD, dim)
    peers_twin = lax.ppermute(peers, "core", swap)
    peers, peers_twin, _ = lax.optimization_barrier((peers, peers_twin, parts))
    parts = exchange(parts, "z")

    whole = jax.ShapeDtypeStruct((grp, rows + PAD, dim), jnp.float32)
    root, root_twin = pl.pallas_call(
        root_kernel,
        out_shape=(whole, whole),
        in_specs=[vmem()] * 2 + [hbm()],
        out_specs=(vmem(), vmem()),
        scratch_shapes=scratch(2, root_own.shape),
        compiler_params=params(),
        cost_estimate=estimate(area, dim),
        name="root_attention",
    )(peers, peers_twin, *in_hbm([root_own]))
    root_twin = lax.ppermute(root_twin.astype(jnp.float16), "core", swap).astype(jnp.float32)
    parts, root, root_twin = lax.optimization_barrier((parts, root, root_twin))
    parts = parts.astype(jnp.float32)
    merged = pl.pallas_call(
        merge_kernel,
        out_shape=whole,
        in_specs=[smem()] + [vmem()] * 3,
        out_specs=vmem(),
        compiler_params=params(),
        name="merge_parts",
    )(readers, parts, root, root_twin)
    back = exchange(merged.astype(jnp.float16), "grp").astype(jnp.float32)
    mine = pl.pallas_call(
        final_kernel,
        out_shape=jax.ShapeDtypeStruct((rows, dim), jnp.bfloat16),
        in_specs=[vmem()] * 2,
        out_specs=vmem(),
        compiler_params=params(),
        name="final_merge",
    )(back, local)
    mine = mine.reshape(heads, steps, group, dim).transpose(1, 0, 2, 3)
    return mine.reshape(queries.shape)


def solution(mesh):
    grp, seq = mesh.devices.shape
    fine = Mesh(mesh.devices.reshape(grp, 2, seq // 4, 2), ("grp", "xhi", "z", "core"))
    seq = ("xhi", "z", "core")
    both = ("grp",) + seq
    in_specs = (
        P(both, None, None, None),
        P(both, None, None),
        P(both, None, None),
        P("grp", seq, None, None),
        P("grp", seq, None, None),
        P(both, None, None, None),
        P(both, None, None, None),
        P(both, None, None, None),
        P(both, None, None, None),
        P(),
        P(),
        P(both),
    )
    out_specs = P(both, None, None, None)
    return jax.shard_map(shards, mesh=fine, in_specs=in_specs, out_specs=out_specs, check_vma=False)
```

```python
import functools
import math

import jax
import jax.numpy as jnp
from jax import lax
from jax.experimental import pallas as pl
from jax.experimental.pallas import tpu as pltpu
from jax.sharding import Mesh, PartitionSpec as P

CAP = 2
PAD = 8
LOW = -1e30
PARTS = 2
EMPHASIS = 20
NT = (((1,), (1,)), ((), ()))


def scores_of(rows, keys):
    raw = lax.dot_general(rows, keys, NT, preferred_element_type=jnp.float32)
    return raw * (1.0 / math.sqrt(keys.shape[-1]))


def raw_weights(rows, keys):
    raw = lax.dot_general(rows, keys, NT, preferred_element_type=jnp.float32)
    top = jnp.max(raw, axis=1, keepdims=True)
    scale = 1.0 / math.sqrt(keys.shape[-1])
    return jnp.exp2((raw - top) * (scale * math.log2(math.e))), top * scale


def times_values(weights, values):
    return jnp.dot(weights.astype(jnp.bfloat16), values, preferred_element_type=jnp.float32)


def head_lse(lse, head, per_head, lanes):
    lse = jnp.broadcast_to(lse, (lse.shape[0], lanes))
    row = lax.broadcasted_iota(jnp.int32, lse.shape, 0)
    col = lax.broadcasted_iota(jnp.int32, lse.shape, 1)
    lse = jnp.where(col == head * per_head + row % per_head, lse, 0.0)
    return jnp.sum(lse.reshape(-1, per_head, lanes), axis=1, keepdims=True)


def tail_rows(pieces):
    shape = pieces[0].shape[:-2] + (PAD, pieces[0].shape[-1])
    row = lax.broadcasted_iota(jnp.int32, shape, len(shape) - 2)
    out = jnp.zeros(shape, jnp.float32)
    for place, piece in enumerate(pieces):
        out = jnp.where(row == place, jnp.broadcast_to(piece, shape), out)
    return out


def split_lse(lse):
    coarse = jnp.round(lse * 0.25) * 4.0
    rest = lse - coarse
    middle = jnp.round(rest * 512.0) * (1.0 / 512.0)
    return coarse, middle, rest - middle


def join_lse(tail):
    return tail[..., 0, :] + tail[..., 1, :] + tail[..., 2, :]


def local_kernel(heads, len_ref, q_ref, k_ref, v_ref, nk_ref, nv_ref, out_ref):
    rows = q_ref.shape[0]
    per_head = rows // heads
    q = q_ref[...]
    far = scores_of(q, k_ref[...])
    row = lax.broadcasted_iota(jnp.int32, far.shape, 0)
    col = lax.broadcasted_iota(jnp.int32, far.shape, 1)
    seen = (col % heads == row // per_head) & (col < len_ref[0] * heads)
    far = jnp.where(seen, far, LOW)
    near = scores_of(q, nk_ref[...])
    row = lax.broadcasted_iota(jnp.int32, near.shape, 0)
    col = lax.broadcasted_iota(jnp.int32, near.shape, 1)
    steps = near.shape[1] // heads
    step = (row % per_head) // (per_head // steps)
    seen = (col % heads == row // per_head) & (col // heads <= step)
    near = jnp.where(seen, near, LOW)
    high = jnp.maximum(
        jnp.max(far, axis=1, keepdims=True), jnp.max(near, axis=1, keepdims=True)
    )
    far = jnp.exp(far - high)
    near = jnp.exp(near - high)
    den = jnp.sum(far, axis=1, keepdims=True) + jnp.sum(near, axis=1, keepdims=True)
    num = times_values(far, v_ref[...]) + times_values(near, nv_ref[...])
    out_ref[:rows, :] = num / den
    lse = jnp.broadcast_to(high + jnp.log(den), (rows, rows))
    row = lax.broadcasted_iota(jnp.int32, (rows, rows), 0)
    col = lax.broadcasted_iota(jnp.int32, (rows, rows), 1)
    flat = jnp.sum(jnp.where(row == col, lse, 0.0), axis=0, keepdims=True)
    out_ref[rows:, :] = jnp.broadcast_to(flat, (PAD, rows))


def select_kernel(idx_ref, peer_ref, out_ref):
    out_ref[...] = jnp.broadcast_to(peer_ref[...][None], out_ref.shape)


def branch_kernel(count, q_ref, *refs):
    sources, out_ref, held, sems = refs[:count], refs[count], refs[count + 1], refs[count + 2]
    slots, lanes, dim = q_ref.shape
    heads = sources[0].shape[0]
    per_head = lanes // heads
    group = heads // PARTS

    def copies(part):
        some = pl.ds(part * group, group)
        return [
            pltpu.make_async_copy(ref.at[some], held.at[place, some], sems.at[place, part])
            for place, ref in enumerate(sources)
        ]

    for part in range(PARTS):
        for place, copy in enumerate(copies(part)):
            copy.start(priority=place % 2)
    tail = jnp.zeros((slots, 1, lanes), jnp.float32)
    for head in range(heads):
        if head % group == 0:
            for copy in copies(head // group):
                copy.wait()
        place = slice(head * per_head, (head + 1) * per_head)
        q = q_ref[:, place, :].reshape(slots * per_head, dim)
        found = []
        for block in range(0, count, 2):
            weights, high = raw_weights(q, held[block, head])
            den = jnp.sum(weights, axis=1, keepdims=True)
            found.append((high, den, times_values(weights, held[block + 1, head])))
        high = functools.reduce(jnp.maximum, [f[0] for f in found])
        factors = [jnp.exp(f[0] - high) for f in found]
        den = sum(factor * f[1] for factor, f in zip(factors, found))
        num = sum(f[2] * (factor / den) for factor, f in zip(factors, found))
        out_ref[:, place, :] = num.reshape(slots, per_head, dim)
        tail = tail + head_lse(high + jnp.log(den), head, per_head, lanes)
    out_ref[:, lanes:, :] = tail_rows(split_lse(tail))


def root_kernel(q_ref, q_twin_ref, block_ref, out_ref, out_twin_ref, held, sems):
    requests, lanes, dim = q_ref.shape
    blocks, heads, half = held.shape[0], held.shape[1], held.shape[2] // 2
    per_head = lanes // heads
    group = heads // PARTS
    span = blocks * half

    def copies(part):
        some = pl.ds(part * group, group)
        cuts = [pl.ds(i * (blocks // 2), blocks // 2) for i in range(2)]
        return [
            pltpu.make_async_copy(
                block_ref.at[cut, some], held.at[cut, some], sems.at[place, part]
            )
            for place, cut in enumerate(cuts)
        ]

    for part in range(PARTS):
        for place, copy in enumerate(copies(part)):
            copy.start(priority=place)
    pairs = ((q_ref, out_ref), (q_twin_ref, out_twin_ref))
    tails = [jnp.zeros((requests, 1, lanes), jnp.float32) for _ in pairs]
    for head in range(heads):
        if head % group == 0:
            for copy in copies(head // group):
                copy.wait()
        place = slice(head * per_head, (head + 1) * per_head)
        keys = held[:, head, :half, :].reshape(span, dim)
        values = held[:, head, half:, :].reshape(span, dim)
        for i, (rows_ref, result_ref) in enumerate(pairs):
            q = rows_ref[:, place, :].reshape(requests * per_head, dim)
            weights, high = raw_weights(q, keys)
            den = jnp.sum(weights, axis=1, keepdims=True)
            num = times_values(weights, values) / den
            result_ref[:, place, :] = num.reshape(requests, per_head, dim)
            tails[i] = tails[i] + head_lse(high + jnp.log(den), head, per_head, lanes)
    for (_, result_ref), tail in zip(pairs, tails):
        result_ref[:, lanes:, :] = tail_rows(split_lse(tail))


def columns(table):
    lanes = table.shape[1]
    rest = jnp.zeros((lanes - table.shape[0], lanes), jnp.float32)
    return jnp.concatenate([table, rest], axis=0).T


def merge_kernel(idx_ref, part_ref, own_ref, twin_ref, out_ref):
    sources, cap, _, lanes = part_ref.shape
    groups = own_ref.shape[0]
    lse_a = join_lse(own_ref[:, lanes:, :])
    lse_b = join_lse(twin_ref[:, lanes:, :])
    high = jnp.maximum(lse_a, lse_b)
    factor_a = jnp.exp(lse_a - high)
    factor_b = jnp.exp(lse_b - high)
    total = factor_a + factor_b
    table = columns(jnp.concatenate([factor_a / total, factor_b / total], axis=0))
    pieces = split_lse(high + jnp.log(total))
    for r in range(groups):
        out_ref[r, :lanes, :] = (
            own_ref[r, :lanes, :] * table[:, r : r + 1]
            + twin_ref[r, :lanes, :] * table[:, groups + r : groups + r + 1]
        )
        out_ref[r, lanes:, :] = tail_rows([piece[r : r + 1] for piece in pieces])
    for k in range(cap):
        reader = idx_ref[k]

        @pl.when(reader >= 0)
        def _():
            lse = join_lse(part_ref[:, k, lanes:, :])
            near = join_lse(out_ref[reader, lanes:, :])[None]
            high = jnp.maximum(jnp.max(lse, axis=0, keepdims=True), near)
            factor = jnp.exp(lse - high)
            near = jnp.exp(near - high)
            total = jnp.sum(factor, axis=0, keepdims=True) + near
            table = columns(jnp.concatenate([factor / total, near / total], axis=0))
            out = out_ref[reader, :lanes, :] * table[:, sources : sources + 1]
            for source in range(sources):
                out = out + part_ref[source, k, :lanes, :] * table[:, source : source + 1]
            out_ref[reader, :lanes, :] = out
            out_ref[reader, lanes:, :] = tail_rows(split_lse(high + jnp.log(total)))


def final_kernel(part_ref, local_ref, out_ref):
    groups, _, lanes = part_ref.shape
    lse = join_lse(part_ref[:, lanes:, :])
    near = local_ref[lanes : lanes + 1, :]
    high = jnp.maximum(jnp.max(lse, axis=0, keepdims=True), near)
    factor = jnp.exp(lse - high)
    near = jnp.exp(near - high)
    total = jnp.sum(factor, axis=0, keepdims=True) + near
    table = columns(jnp.concatenate([factor / total, near / total], axis=0))
    out = local_ref[:lanes, :] * table[:, groups : groups + 1]
    for source in range(groups):
        out = out + part_ref[source, :lanes, :] * table[:, source : source + 1]
    out_ref[...] = out.astype(out_ref.dtype)


def params(megabytes=20):
    return pltpu.CompilerParams(vmem_limit_bytes=megabytes * 1024 * 1024)


def estimate(area, dim, emphasis=1):
    return pl.CostEstimate(
        flops=emphasis * 4 * area * dim, bytes_accessed=6 * 1024 * 1024, transcendentals=area
    )


def vmem():
    return pl.BlockSpec(memory_space=pltpu.VMEM)


def hbm():
    return pl.BlockSpec(memory_space=pltpu.HBM)


def smem():
    return pl.BlockSpec(memory_space=pltpu.SMEM)


def scratch(count, shape):
    return [pltpu.VMEM(shape, jnp.bfloat16), pltpu.SemaphoreType.DMA((count, PARTS))]


def in_hbm(blocks):
    return [pltpu.with_memory_space_constraint(block, pltpu.HBM) for block in blocks]


def exchange(blocks, axis):
    return lax.all_to_all(blocks, axis, split_axis=0, concat_axis=0, tiled=True)


def to_all(block, axis):
    return exchange(jnp.broadcast_to(block[None], (lax.axis_size(axis),) + block.shape), axis)


def shards(
    queries,
    root_keys,
    root_values,
    branch_keys,
    branch_values,
    suffix_keys,
    suffix_values,
    new_keys,
    new_values,
    branch_of,
    owner,
    suffix_len,
):
    steps, q_heads, dim = queries.shape[1:]
    heads = root_keys.shape[1]
    group = q_heads // heads
    per_head = steps * group
    rows = heads * per_head
    grp = lax.axis_size("grp")
    ring = lax.axis_size("z")
    core = lax.axis_size("core")
    spots = lax.axis_size("xhi") * ring * core
    grp_place = lax.axis_index("grp")
    seq_place = (lax.axis_index("xhi") * ring + lax.axis_index("z")) * core + lax.axis_index("core")
    swap = [(0, 1), (1, 0)]

    q_rows = queries[0].reshape(steps, heads, group, dim).transpose(1, 0, 2, 3)
    q_rows = q_rows.reshape(rows, dim)
    peers = to_all(q_rows, "grp")

    matches = branch_of[:, None] == jnp.arange(owner.shape[0])[None, :]
    slot_of = jnp.sum(jnp.where(matches, owner[None, :], 0), axis=1)
    slot_here = lax.dynamic_slice_in_dim(slot_of.reshape(grp, spots), seq_place, 1, 1)[:, 0]
    reading = slot_here == grp_place
    group_ids = jnp.arange(grp)
    before = jnp.sum((reading[None, :] & (group_ids[None, :] < group_ids[:, None])), axis=1)
    chosen = reading[None, :] & (before[None, :] == jnp.arange(CAP)[:, None])
    readers = jnp.max(jnp.where(chosen, group_ids[None, :], -1), axis=1).astype(jnp.int32)

    area = ring * CAP * rows * branch_keys.shape[1] * 4

    def gather_readers(peers):
        packed = pl.pallas_call(
            select_kernel,
            out_shape=jax.ShapeDtypeStruct((ring, CAP, rows, dim), jnp.bfloat16),
            grid_spec=pltpu.PrefetchScalarGridSpec(
                num_scalar_prefetch=1,
                grid=(CAP,),
                in_specs=[
                    pl.BlockSpec((1, rows, dim), lambda k, idx: (jnp.maximum(idx[k], 0), 0, 0))
                ],
                out_specs=pl.BlockSpec((ring, 1, rows, dim), lambda k, idx: (0, k, 0, 0)),
            ),
            compiler_params=params(),
            cost_estimate=estimate(area, dim, EMPHASIS),
            name="pick_readers",
        )(readers, peers)
        return exchange(packed, "z")

    root_block = jnp.concatenate([root_keys, root_values], axis=0).transpose(1, 0, 2)
    pair = jnp.stack([root_block, lax.ppermute(root_block, "xhi", swap)])
    pair, keys_own, values_own = lax.optimization_barrier((pair, branch_keys[0], branch_values[0]))
    root_own = lax.all_gather(pair, "z", axis=0, tiled=True)
    keys_own = keys_own.transpose(1, 0, 2)
    values_own = values_own.transpose(1, 0, 2)
    peers, _ = lax.optimization_barrier((peers, pair))
    keys_far = lax.ppermute(keys_own, "xhi", swap)
    values_far = lax.ppermute(values_own, "xhi", swap)
    slots = gather_readers(peers)
    branch_blocks = [
        keys_own,
        values_own,
        lax.ppermute(keys_own, "core", swap),
        lax.ppermute(values_own, "core", swap),
        keys_far,
        values_far,
        lax.ppermute(keys_far, "core", swap),
        lax.ppermute(values_far, "core", swap),
    ]
    flat = suffix_keys.shape[1] * heads
    local = pl.pallas_call(
        functools.partial(local_kernel, heads),
        out_shape=jax.ShapeDtypeStruct((rows + PAD, dim), jnp.float32),
        in_specs=[smem()] + [vmem()] * 5,
        out_specs=vmem(),
        compiler_params=params(),
        cost_estimate=pl.CostEstimate(
            flops=4 * rows * flat * dim, bytes_accessed=4 * flat * dim, transcendentals=rows * flat
        ),
        name="local_attention",
    )(
        suffix_len,
        q_rows,
        suffix_keys.reshape(flat, dim),
        suffix_values.reshape(flat, dim),
        new_keys.reshape(steps * heads, dim),
        new_values.reshape(steps * heads, dim),
    )

    slots = slots.reshape(ring * CAP, rows, dim)
    area = ring * CAP * rows * branch_keys.shape[1] * 4
    count = len(branch_blocks)
    parts = pl.pallas_call(
        functools.partial(branch_kernel, count),
        out_shape=jax.ShapeDtypeStruct((ring * CAP, rows + PAD, dim), jnp.float32),
        in_specs=[vmem()] + [hbm()] * count,
        out_specs=vmem(),
        scratch_shapes=scratch(count, (count,) + keys_own.shape),
        compiler_params=params(),
        cost_estimate=estimate(area, dim),
        name="branch_attention",
    )(slots, *in_hbm(branch_blocks))
    parts = parts.astype(jnp.float16).reshape(ring, CAP, rows + PAD, dim)
    peers_twin = lax.ppermute(peers, "core", swap)
    peers, peers_twin, _ = lax.optimization_barrier((peers, peers_twin, parts))
    parts = exchange(parts, "z")

    whole = jax.ShapeDtypeStruct((grp, rows + PAD, dim), jnp.float32)
    root, root_twin = pl.pallas_call(
        root_kernel,
        out_shape=(whole, whole),
        in_specs=[vmem()] * 2 + [hbm()],
        out_specs=(vmem(), vmem()),
        scratch_shapes=scratch(2, root_own.shape),
        compiler_params=params(),
        cost_estimate=estimate(area, dim),
        name="root_attention",
    )(peers, peers_twin, *in_hbm([root_own]))
    root_twin = lax.ppermute(root_twin.astype(jnp.float16), "core", swap).astype(jnp.float32)
    parts, root, root_twin = lax.optimization_barrier((parts, root, root_twin))
    parts = parts.astype(jnp.float32)
    merged = pl.pallas_call(
        merge_kernel,
        out_shape=whole,
        in_specs=[smem()] + [vmem()] * 3,
        out_specs=vmem(),
        compiler_params=params(),
        name="merge_parts",
    )(readers, parts, root, root_twin)
    back = exchange(merged.astype(jnp.float16), "grp").astype(jnp.float32)
    mine = pl.pallas_call(
        final_kernel,
        out_shape=jax.ShapeDtypeStruct((rows, dim), jnp.bfloat16),
        in_specs=[vmem()] * 2,
        out_specs=vmem(),
        compiler_params=params(),
        name="final_merge",
    )(back, local)
    mine = mine.reshape(heads, steps, group, dim).transpose(1, 0, 2, 3)
    return mine.reshape(queries.shape)


def solution(mesh):
    grp, seq = mesh.devices.shape
    fine = Mesh(mesh.devices.reshape(grp, 2, seq // 4, 2), ("grp", "xhi", "z", "core"))
    seq = ("xhi", "z", "core")
    both = ("grp",) + seq
    in_specs = (
        P(both, None, None, None),
        P(both, None, None),
        P(both, None, None),
        P("grp", seq, None, None),
        P("grp", seq, None, None),
        P(both, None, None, None),
        P(both, None, None, None),
        P(both, None, None, None),
        P(both, None, None, None),
        P(),
        P(),
        P(both),
    )
    out_specs = P(both, None, None, None)
    return jax.shard_map(shards, mesh=fine, in_specs=in_specs, out_specs=out_specs, check_vma=False)
```
